768 devices in a mesh: dp: 96 (over z, x, core), lists: 8 (over y).
Axes of the slice: x: 4, y: 8, z: 12, core: 2. Of those that a mesh axis runs over, the one named last changes fastest.
Arguments:
- pooled: bfloat16 [196608, 4096], P(('dp', 'lists')), may hold values from -6 to 6
- proj_weight: bfloat16 [4096, 1024], replicated, may hold values from -0.09375 to 0.09375
- centroids: bfloat16 [49152, 1024], P(('dp', 'lists')), may hold values from -6 to 6
- list_slot: int32 [196608], P(('dp', 'lists')), may hold values from 0 to 63
- pq_codes: int32 [196608, 64], P(('dp', 'lists')), may hold values from 0 to 255
- route_counts: int32 [768, 8], P(('dp', 'lists')), may hold values from 1 to 64, as said below
Outputs:
- new_centroids: float32 [49152, 1024], P(('dp', 'lists'))
- codebook: float32 [64, 16, 256], P('lists')
The draws below stay inside these ranges and needn't reach their ends.
Inputs may be any that keep to these rules, and one draw needn't show every extreme that they name: `route_counts`: row b gives how many rows of device block b, in order, go to each lists index of its dp group; each row sums to 256 and holds one entry equal to 64, at the same position for all blocks of one dp index.
All inputs are finite; a program needn't handle non-finite values.
Results may differ from the reference program's by a relative error of at most 0.0038.
Values may be sent and summed in bfloat16 or wider, within the bound.
A program may use at most 64 MiB of HBM per device.

```python
import jax
import jax.numpy as jnp
from jax import lax

DIN = 4096
D = 1024
SUB = 64
CODES = 256
SUBW = 16
LIST_DEV = 64
ROW_DEV = 256
CAP = 64
ROWS = 196608
LISTS = 49152
N_DP = 96
N_LISTS = 8


def draw_route_counts(key, part):
    key = jax.random.fold_in(key, 7)
    hot_key, pair_key, order_key = jax.random.split(key, 3)
    owners = N_LISTS
    rows_all = N_DP * N_LISTS
    spare = ROW_DEV - CAP
    base = spare // (owners - 1)
    extra = spare - base * (owners - 1)
    others = base + (jnp.arange(owners - 1, dtype=jnp.int32) < extra).astype(jnp.int32)
    others = jnp.broadcast_to(others[None, :], (rows_all, owners - 1))
    pair_count = (owners - 1) // 2
    spread = max(0, min(base - 1, CAP - base - 2))
    moves = jax.random.randint(pair_key, (rows_all, pair_count), 0, spread + 1, dtype=jnp.int32)
    shifted = jnp.stack([-moves, moves], axis=2).reshape(rows_all, 2 * pair_count)
    if 2 * pair_count < owners - 1:
        shifted = jnp.concatenate([shifted, jnp.zeros((rows_all, 1), jnp.int32)], axis=1)
    others = others + shifted
    scores = jax.random.randint(order_key, (rows_all, owners - 1), 0, 1 << 20, dtype=jnp.int32) * owners
    scores = scores + jnp.arange(owners - 1, dtype=jnp.int32)[None, :]
    order = jnp.argsort(scores, axis=1)
    others = jnp.take_along_axis(others, order, axis=1)
    hot = jax.random.randint(hot_key, (N_DP,), 0, owners, dtype=jnp.int32)
    hot_rows = jnp.repeat(hot, owners)[:, None]
    column = jnp.arange(owners, dtype=jnp.int32)[None, :]
    pick = jnp.clip(column - (column > hot_rows).astype(jnp.int32), 0, owners - 2)
    values = jnp.take_along_axis(others, jnp.broadcast_to(pick, (rows_all, owners)), axis=1)
    return jnp.where(column == hot_rows, CAP, values).astype(jnp.int32)


def with_ends(result, rng, low, high):
    longest = result.shape.index(max(result.shape))
    spots = []
    for shift in (0, 1):
        where = [jax.random.randint(jax.random.fold_in(rng, axis), (), 0, length) for axis, length in enumerate(result.shape)]
        where[longest] = (where[longest] + shift) % result.shape[longest]
        spots.append(tuple(where))
    return result.at[spots[0]].set(low).at[spots[1]].set(high)


def block_scale(stream_key, shape, cuts, low, top_value):
    loudness = 1.0
    for position, blocks in cuts:
        draws = jax.random.uniform(jax.random.fold_in(jax.random.fold_in(stream_key, 6), position), (blocks,), jnp.float32, low / len(cuts), top_value / len(cuts))
        loudness = loudness * jnp.repeat(jnp.exp(draws), shape[position] // blocks).reshape((-1,) + (1,) * (len(shape) - 1 - position))
    return loudness


def normal_values(key, dims, width, most, shards=(), kind=jnp.bfloat16):
    values = width * jax.random.normal(key, dims, jnp.float32)
    if shards:
        values = values * block_scale(key, dims, shards, -0.22, 0.18)
    return jnp.clip(values, -most, most).astype(kind)


def setup_inputs(seed: int = 0) -> dict:
    arg_keys = jax.random.split(jax.random.key(seed), 7)
    return {
        "pooled": normal_values(arg_keys[0], (ROWS, DIN), 1.0, 6.0, ((0, 768),)),
        "proj_weight": normal_values(arg_keys[1], (DIN, D), DIN ** -0.5, 0.09375),
        "centroids": normal_values(arg_keys[2], (LISTS, D), 1.0, 6.0, ((0, 768),)),
        "list_slot": with_ends(jax.random.randint(arg_keys[3], (ROWS,), 0, LIST_DEV), jax.random.fold_in(arg_keys[3], 1), 0, LIST_DEV - 1).astype(jnp.int32),
        "pq_codes": with_ends(jax.random.randint(arg_keys[4], (ROWS, SUB), 0, CODES), jax.random.fold_in(arg_keys[4], 1), 0, CODES - 1).astype(jnp.int32),
        "route_counts": draw_route_counts(jax.random.fold_in(arg_keys[6], 71), 0),
    }


def reference(pooled, proj_weight, centroids, list_slot, pq_codes, route_counts):
    projected = jnp.dot(pooled, proj_weight, preferred_element_type=jnp.float32)
    factor = lax.rsqrt(lax.optimization_barrier(jnp.mean(projected * projected, axis=1, keepdims=True)) + 1e-06)
    normed = (projected * factor).astype(jnp.bfloat16)
    normed_wide = normed.astype(jnp.float32)
    blocks = route_counts.shape[0]
    ends = jnp.cumsum(route_counts, axis=1)
    positions = jnp.arange(ROW_DEV, dtype=jnp.int32)
    target = lax.optimization_barrier(jnp.sum((positions[None, :, None] >= ends[:, None, :]).astype(jnp.int32), axis=2))
    groups = (jnp.arange(blocks, dtype=jnp.int32) // N_LISTS)[:, None]
    list_index = ((groups * N_LISTS + target) * LIST_DEV + list_slot.reshape(blocks, ROW_DEV)).reshape(-1).astype(jnp.int32)
    assigned = centroids[list_index].astype(jnp.float32)
    residual = (normed_wide - assigned).astype(jnp.bfloat16)
    ones_rows = jnp.ones((normed.shape[0],), jnp.float32)
    list_sums = jax.ops.segment_sum(normed_wide, list_index, num_segments=LISTS)
    list_tally = jax.ops.segment_sum(ones_rows, list_index, num_segments=LISTS)
    new_centroids = (centroids.astype(jnp.float32) + list_sums) / (1.0 + list_tally)[:, None]
    pieces = residual.astype(jnp.float32).reshape(-1, SUBW)
    code_ids = (pq_codes + CODES * jnp.arange(SUB, dtype=jnp.int32)[None, :]).reshape(-1).astype(jnp.int32)
    ones_pieces = jnp.ones((pieces.shape[0],), jnp.float32)
    code_sums = jax.ops.segment_sum(pieces, code_ids, num_segments=SUB * CODES)
    code_tally = jax.ops.segment_sum(ones_pieces, code_ids, num_segments=SUB * CODES)
    code_sums = code_sums.reshape(SUB, CODES, SUBW).transpose(0, 2, 1)
    codebook = code_sums / (1.0 + code_tally.reshape(SUB, CODES))[:, None, :]
    return (new_centroids, codebook)
```

```python
import functools

import jax
import jax.numpy as jnp
from jax import lax
from jax.experimental import pallas as pl
from jax.experimental.pallas import tpu as pltpu
from jax.sharding import PartitionSpec as P

SUB = 64
CODES = 256
SUBW = 16
CAP = 64
LANES = 128
MESH = pl.DeviceIdType.MESH
BF = jnp.bfloat16
F32 = jnp.float32
I32 = jnp.int32
K_PARTS = 4


def iota(shape, dim):
    return lax.broadcasted_iota(I32, shape, dim)


def hot(mask):
    return jnp.where(mask, 1.0, 0.0).astype(BF)


def dot(a, b):
    return jnp.dot(a, b, preferred_element_type=F32)


def dot_nt(a, b):
    return lax.dot_general(a, b, (((1,), (1,)), ((), ())), preferred_element_type=F32)


def kernel(
    n_z, n_xc, n_y,
    counts_ref, slot_ref, codes_ref, cent_ref, pooled_hbm, weight_hbm,
    newc_ref, book_ref,
    pooled_v, weight_v, normed_v, xt_v, call_v, own_v, res_v,
    tl_v, t1_r, t2_b, t2_r, t3_r,
    cd_b, cd_r, ls_b, ls_r, s1_b, s1_r, s2_b, s2_r, s3_r, s4_r,
    in_sem, tl_s, t2_s, t3_s, cd_s, ls_s, s1_s, s2_s, s3_s, s4_s,
):
    rows, features = normed_v.shape[0], res_v.shape[1]
    dp, y = lax.axis_index("dp"), lax.axis_index("lists")
    z, xc = dp // n_xc, dp % n_xc

    def at_xc(o):
        return z * n_xc + lax.rem(xc + o, n_xc)

    def at_y(o):
        return lax.rem(y + o, n_y)

    def at_z(o):
        return lax.rem(z + o, n_z) * n_xc + xc

    def send(src, dst, sems, o, device):
        return pltpu.make_async_remote_copy(
            src_ref=src, dst_ref=dst, send_sem=sems.at[0, o], recv_sem=sems.at[1, o],
            device_id=device, device_id_type=MESH,
        )

    def tally1(o):
        return send(tl_v.at[lax.rem(xc + o, n_xc)], t1_r.at[o], tl_s, o, (at_xc(o), y))

    def tally2(o):
        return send(t2_b.at[at_y(o)], t2_r.at[o], t2_s, o, (dp, at_y(o)))

    def tally3(o):
        return send(t3_r.at[z], t3_r.at[z], t3_s, o, (at_z(o), y))

    def codes_out(o):
        return send(cd_b.at[at_y(o)], cd_r.at[o], cd_s, o, (dp, at_y(o)))

    def lists_out(o):
        block = pl.ds(pl.multiple_of(at_y(o) * CAP, CAP), CAP)
        return send(ls_b.at[block], ls_r.at[o], ls_s, o, (dp, at_y(o)))

    def sums1(o):
        return send(s1_b.at[o], s1_r.at[o], s1_s, o, (at_xc(o), y))

    def sums2(o):
        return send(s2_b.at[at_y(o)], s2_r.at[o], s2_s, o, (dp, at_y(o)))

    def sums3(o):
        return send(s3_r.at[z], s3_r.at[z], s3_s, o, (at_z(o), y))

    def sums4(o):
        return send(s4_r.at[xc], s4_r.at[xc], s4_s, o, (at_xc(o), y))

    depth = weight_v.shape[1]
    loads = []
    for k in range(K_PARTS):
        cols = pl.ds(k * depth, depth)
        pair = (
            pltpu.make_async_copy(pooled_hbm.at[:, cols], pooled_v.at[k], in_sem.at[0, k]),
            pltpu.make_async_copy(weight_hbm.at[cols], weight_v.at[k], in_sem.at[1, k]),
        )
        for copy in pair:
            copy.start()
        loads.append(pair)

    barrier = pltpu.get_barrier_semaphore()
    for o in range(1, n_xc):
        pl.semaphore_signal(barrier, inc=1, device_id=(at_xc(o), y), device_id_type=MESH)
    for o in range(1, n_y):
        pl.semaphore_signal(barrier, inc=1, device_id=(dp, at_y(o)), device_id_type=MESH)
    for o in range(1, n_z):
        pl.semaphore_signal(barrier, inc=1, device_id=(at_z(o), y), device_id_type=MESH)

    slot = slot_ref[...]
    pos = iota((1, rows), 1)
    target = jnp.zeros((1, rows), I32)
    lane = iota((rows, LANES), 1) - (y % 2) * CAP
    row = iota((rows, LANES), 0)
    start = 0
    places = []
    for d in range(n_y):
        count = counts_ref[0, d]
        places.append(hot((row == lane + start) & (lane >= 0) & (lane < count)))
        start = start + count
        target = target + jnp.where(pos >= start, 1, 0)
    codes = codes_ref[...]
    extra = jnp.where(iota((16, rows), 0) == 0, slot + 1, 0)
    packed = dot(
        jnp.concatenate([codes, extra], 0).astype(F32).astype(BF), jnp.concatenate(places, 1)
    ).astype(BF)
    for d in range(n_y):
        cd_b[d] = packed[:, d * LANES : (d + 1) * LANES]

    r128, l128 = iota((LANES, LANES), 0), iota((LANES, LANES), 1)
    rep = hot(iota((LANES, CODES), 0) % 16 == iota((LANES, CODES), 1) % 16)
    pick = iota((LANES, CODES), 0) % 16 == iota((LANES, CODES), 1) // 16
    fold = hot(iota((8, LANES), 1) // 16 == iota((8, LANES), 0))
    step = iota((LANES, rows), 0) % 16
    for g in range(SUB // 8):
        wide = jnp.concatenate(
            [jnp.broadcast_to(codes[g * 8 + j : g * 8 + j + 1], (16, rows)) for j in range(8)], 0
        )
        pairs = dot_nt(hot(wide // 16 == step), hot(wide % 16 == step))
        pairs = jnp.where(r128 // 16 == l128 // 16, pairs, 0.0).astype(BF)
        spread = jnp.where(pick, dot(pairs, rep), 0.0).astype(BF)
        tally = dot(fold, spread)
        for j in range(8):
            tl_v[j, g : g + 1] = tally[j : j + 1]

    pl.semaphore_wait(barrier, n_xc + n_y + n_z - 3)
    for o in range(1, n_y):
        codes_out(o).start()
    for o in range(1, n_xc):
        tally1(o).start()

    for k in range(K_PARTS):
        for copy in loads[k]:
            copy.wait()
        part = dot(pooled_v[k], weight_v[k])
        if k == 0:
            res_v[...] = part
        else:
            res_v[...] += part
    acc = res_v[...]
    factor = lax.rsqrt(jnp.mean(acc * acc, axis=1, keepdims=True) + 1e-6)
    normed = (acc * factor).astype(BF)
    normed_v[:, :features] = normed
    normed_v[:, features:] = jnp.ones((rows, LANES), BF)

    group_list = target * CAP + slot
    ls_b[...] = dot(hot(iota((n_y * CAP, rows), 0) == group_list), normed_v[...]).astype(BF)
    for o in range(1, n_y):
        lists_out(o).start()

    xt_v[:, :rows] = normed_v[:, :features].T
    call_v[:, :rows] = codes

    own = tl_v[xc]
    for o in range(1, n_xc):
        tally1(o).wait_recv()
        own = own + t1_r[o]
    for d in range(n_y):
        t2_b[d] = own[d : d + 1]
    for o in range(1, n_y):
        tally2(o).start()

    cd_r[0] = cd_b[y]
    for o in range(1, n_y):
        codes_out(o).wait_recv()
    for p in range(n_y // 2):
        both = cd_r[2 * p].astype(F32) + cd_r[2 * p + 1].astype(F32)
        cols = slice(rows + p * LANES, rows + (p + 1) * LANES)
        call_v[:, cols] = both[:SUB].astype(I32)
        chosen = hot(iota((CAP, LANES), 0) + 1 == both[SUB : SUB + 1].astype(I32))
        minus = lax.dot_general(
            cent_ref[...], chosen, (((0,), (0,)), ((), ())), preferred_element_type=F32
        )
        xt_v[:, cols] = (-minus).astype(BF)

    all_rows = call_v.shape[1]
    low = iota((16, all_rows), 0)

    def code_sums(o, out, kind):
        dest = lax.rem(xc + o, n_xc)
        for d in range(n_y):
            m = d * n_xc + dest
            gap = jnp.broadcast_to(call_v[pl.ds(m, 1)], (16, all_rows)) - low
            select = jnp.concatenate([hot(gap == 16 * h) for h in range(CODES // 16)], 0)
            piece = xt_v[pl.ds(pl.multiple_of(m * SUBW, SUBW), SUBW)]
            out[d * SUBW : (d + 1) * SUBW] = dot_nt(piece, select).astype(kind)

    def remote_chunk(o, carry):
        code_sums(o, s1_b.at[o], BF)
        sums1(o).start()
        return carry

    lax.fori_loop(1, n_xc, remote_chunk, 0)
    code_sums(0, own_v, F32)

    total = t2_b[y]
    for o in range(1, n_y):
        tally2(o).wait_recv()
        total = total + t2_r[o]
    t3_r[z] = total
    for o in range(1, n_z):
        tally3(o).start()

    for o in range(1, n_xc):
        sums1(o).wait_recv()
    for d in range(n_y):
        part = slice(d * SUBW, (d + 1) * SUBW)
        run = own_v[part]
        for o in range(1, n_xc):
            run = run + s1_r[o, part].astype(F32)
        s2_b[d] = run
    for o in range(1, n_y):
        sums2(o).start()
    run = s2_b[y]
    for o in range(1, n_y):
        sums2(o).wait_recv()
        run = run + s2_r[o]
    s3_r[z] = run.astype(BF)
    for o in range(1, n_z):
        sums3(o).start()

    for o in range(1, n_y):
        lists_out(o).wait_recv()
    lists = ls_b[pl.ds(pl.multiple_of(y * CAP, CAP), CAP)].astype(F32)
    for o in range(1, n_y):
        lists = lists + ls_r[o].astype(F32)
    scale = 1.0 / (1.0 + lists[:, features : features + 1])
    newc_ref[...] = (cent_ref[...].astype(F32) + lists[:, :features]) * scale

    for o in range(1, n_z):
        tally3(o).wait_recv()
    for o in range(1, n_z):
        sums3(o).wait_recv()
    total, run = t3_r[0], s3_r[0].astype(F32)
    for i in range(1, n_z):
        total = total + t3_r[i]
        run = run + s3_r[i].astype(F32)
    s4_r[xc] = run / (1.0 + total)
    for o in range(1, n_xc):
        sums4(o).start()
    for o in range(1, n_xc):
        sums4(o).wait_recv()
    book_ref[...] = s4_r[...]

    for o in range(1, n_xc):
        tally1(o).wait_send()
        sums1(o).wait_send()
        sums4(o).wait_send()
    for o in range(1, n_y):
        codes_out(o).wait_send()
        lists_out(o).wait_send()
        tally2(o).wait_send()
        sums2(o).wait_send()
    for o in range(1, n_z):
        tally3(o).wait_send()
        sums3(o).wait_send()


def local(n_z, n_xc, pooled, proj_weight, centroids, list_slot, pq_codes, route_counts):
    n_y = lax.axis_size("lists")
    rows, din = pooled.shape
    features = proj_weight.shape[1]
    all_rows = rows + n_y * CAP
    wide = features + LANES
    share = SUB // n_y
    depth = din // K_PARTS
    sem = pltpu.SemaphoreType.DMA
    vmem = pl.BlockSpec(memory_space=pltpu.VMEM)
    return pl.pallas_call(
        functools.partial(kernel, n_z, n_xc, n_y),
        out_shape=(
            jax.ShapeDtypeStruct(centroids.shape, F32),
            jax.ShapeDtypeStruct((share, SUBW, CODES), F32),
        ),
        in_specs=[
            pl.BlockSpec(memory_space=pltpu.SMEM), vmem, vmem, vmem,
            pl.BlockSpec(memory_space=pl.ANY), pl.BlockSpec(memory_space=pl.ANY),
        ],
        out_specs=(vmem, vmem),
        scratch_shapes=[
            pltpu.VMEM((K_PARTS, rows, depth), BF),
            pltpu.VMEM((K_PARTS, depth, features), BF),
            pltpu.VMEM((rows, wide), BF),
            pltpu.VMEM((features, all_rows), BF),
            pltpu.VMEM((SUB, all_rows), I32),
            pltpu.VMEM((n_y * SUBW, CODES), F32),
            pltpu.VMEM((rows, features), F32),
            pltpu.VMEM((n_xc, n_y, CODES), F32),
            pltpu.VMEM((n_xc, n_y, CODES), F32),
            pltpu.VMEM((n_y, 1, CODES), F32),
            pltpu.VMEM((n_y, 1, CODES), F32),
            pltpu.VMEM((n_z, 1, CODES), F32),
            pltpu.VMEM((n_y, SUB + 16, LANES), BF),
            pltpu.VMEM((n_y, SUB + 16, LANES), BF),
            pltpu.VMEM((n_y * CAP, wide), BF),
            pltpu.VMEM((n_y, CAP, wide), BF),
            pltpu.VMEM((n_xc, n_y * SUBW, CODES), BF),
            pltpu.VMEM((n_xc, n_y * SUBW, CODES), BF),
            pltpu.VMEM((n_y, SUBW, CODES), F32),
            pltpu.VMEM((n_y, SUBW, CODES), F32),
            pltpu.VMEM((n_z, SUBW, CODES), BF),
            pltpu.VMEM((n_xc, SUBW, CODES), F32),
            sem((2, K_PARTS)), sem((2, n_xc)), sem((2, n_y)), sem((2, n_z)), sem((2, n_y)),
            sem((2, n_y)), sem((2, n_xc)), sem((2, n_y)), sem((2, n_z)), sem((2, n_xc)),
        ],
        compiler_params=pltpu.CompilerParams(
            collective_id=0, has_side_effects=True, vmem_limit_bytes=48 << 20
        ),
        name="step",
    )(route_counts, list_slot.reshape(1, rows), pq_codes.T, centroids, pooled, proj_weight)


def solution(mesh):
    n_xc = SUB // mesh.shape["lists"]
    in_specs = (
        P(("dp", "lists"), None),
        P(),
        P(("dp", "lists"), None),
        P(("dp", "lists")),
        P(("dp", "lists"), None),
        P(("dp", "lists"), None),
    )
    out_specs = (P(("dp", "lists"), None), P("lists", None, None))
    step = functools.partial(local, mesh.shape["dp"] // n_xc, n_xc)
    return jax.shard_map(step, mesh=mesh, in_specs=in_specs, out_specs=out_specs, check_vma=False)
```

```python
import functools

import jax
import jax.numpy as jnp
from jax import lax
from jax.experimental import pallas as pl
from jax.experimental.pallas import tpu as pltpu
from jax.sharding import PartitionSpec as P

SUB = 64
CODES = 256
SUBW = 16
CAP = 64
LANES = 128
MESH = pl.DeviceIdType.MESH
BF = jnp.bfloat16
F32 = jnp.float32
I32 = jnp.int32
K_PARTS = 4


def iota(shape, dim):
    return lax.broadcasted_iota(I32, shape, dim)


def hot(mask):
    return jnp.where(mask, 1.0, 0.0).astype(BF)


def dot(a, b):
    return jnp.dot(a, b, preferred_element_type=F32)


def dot_nt(a, b):
    return lax.dot_general(a, b, (((1,), (1,)), ((), ())), preferred_element_type=F32)


def kernel(
    n_z, n_xc, n_y,
    counts_hbm, slot_hbm, codes_hbm, cent_hbm, pooled_hbm, weight_hbm,
    newc_ref, book_ref,
    counts_ref, slot_ref, codes_ref, cent_ref,
    pooled_v, weight_v, normed_v, xt_v, call_v, own_v, res_v,
    tl_v, t1_r, t2_b, t2_r, t3_r,
    cd_b, cd_r, ls_b, up_r, down_r, tally_v, s1_b, s1_r, s2_b, s2_r, s3_r, s4_r,
    in_sem, small_sem, tl_s, t2_s, t3_s, cd_s, up_s, down_s, s1_s, s2_s, s3_s, s4_s,
):
    rows, features = normed_v.shape[0], res_v.shape[1]
    dp, y = lax.axis_index("dp"), lax.axis_index("lists")
    z, xc = dp // n_xc, dp % n_xc

    def at_xc(o):
        return z * n_xc + lax.rem(xc + o, n_xc)

    def at_y(o):
        return lax.rem(y + o, n_y)

    def at_z(o):
        return lax.rem(z + o, n_z) * n_xc + xc

    def send(src, dst, sems, o, device):
        return pltpu.make_async_remote_copy(
            src_ref=src, dst_ref=dst, send_sem=sems.at[0, o], recv_sem=sems.at[1, o],
            device_id=device, device_id_type=MESH,
        )

    def tally1(o):
        return send(tl_v.at[lax.rem(xc + o, n_xc)], t1_r.at[o], tl_s, o, (at_xc(o), y))

    def tally2(o):
        return send(t2_b.at[at_y(o)], t2_r.at[o], t2_s, o, (dp, at_y(o)))

    def tally3(o):
        return send(t3_r.at[z], t3_r.at[z], t3_s, o, (at_z(o), y))

    def codes_out(o):
        return send(cd_b.at[at_y(o)], cd_r.at[o], cd_s, o, (dp, at_y(o)))

    far = n_y // 2
    half = features // 2

    def block(o):
        return pl.ds(pl.multiple_of(at_y(o) * CAP, CAP), CAP)

    def ring(s, up):
        dest = block(far + 1 - s if up else n_y - far - 1 + s)
        slots, sems = (up_r, up_s) if up else (down_r, down_s)
        src, dst = ls_b.at[dest], slots.at[s - 1]
        if s == 1:
            cols = pl.ds(0 if up else half, half)
            src, dst = src.at[:, cols], dst.at[:, cols]
        return send(src, dst, sems, s - 1, (dp, at_y(1 if up else n_y - 1)))

    def ring_step(s):
        for up in (True, False):
            ring(s - 1, up).wait_recv()
            dest = block(far + 1 - s if up else n_y - far - 1 + s)
            cols = slice(0, features)
            if s == 2:
                cols = slice(0, half) if up else slice(half, features)
            came = (up_r if up else down_r)[s - 2, :, cols].astype(F32)
            ls_b[dest, cols] = (ls_b[dest, cols].astype(F32) + came).astype(BF)
            ring(s, up).start()

    def sums1(o):
        return send(s1_b.at[o], s1_r.at[o], s1_s, o, (at_xc(o), y))

    def sums2(o):
        return send(s2_b.at[at_y(o)], s2_r.at[o], s2_s, o, (dp, at_y(o)))

    def sums3(o):
        return send(s3_r.at[z], s3_r.at[z], s3_s, o, (at_z(o), y))

    def sums4(o):
        return send(s4_r.at[xc], s4_r.at[xc], s4_s, o, (at_xc(o), y))

    small = [
        pltpu.make_async_copy(src, dst, small_sem.at[i])
        for i, (src, dst) in enumerate(
            (
                (counts_hbm, counts_ref),
                (slot_hbm, slot_ref),
                (codes_hbm, codes_ref),
                (cent_hbm, cent_ref),
            )
        )
    ]
    for copy in small:
        copy.start()
    depth = weight_v.shape[1]
    loads = []
    for k in range(K_PARTS):
        cols = pl.ds(k * depth, depth)
        pair = (
            pltpu.make_async_copy(pooled_hbm.at[:, cols], pooled_v.at[k], in_sem.at[0, k]),
            pltpu.make_async_copy(weight_hbm.at[cols], weight_v.at[k], in_sem.at[1, k]),
        )
        for copy in pair:
            copy.start()
        loads.append(pair)

    barrier = pltpu.get_barrier_semaphore()
    for o in range(1, n_xc):
        pl.semaphore_signal(barrier, inc=1, device_id=(at_xc(o), y), device_id_type=MESH)
    for o in range(1, n_y):
        pl.semaphore_signal(barrier, inc=1, device_id=(dp, at_y(o)), device_id_type=MESH)
    for o in range(1, n_z):
        pl.semaphore_signal(barrier, inc=1, device_id=(at_z(o), y), device_id_type=MESH)

    for copy in small:
        copy.wait()
    slot = slot_ref[...]
    pos = iota((1, rows), 1)
    target = jnp.zeros((1, rows), I32)
    lane = iota((rows, LANES), 1) - (y % 2) * CAP
    row = iota((rows, LANES), 0)
    start = 0
    places = []
    for d in range(n_y):
        count = counts_ref[0, d]
        places.append(hot((row == lane + start) & (lane >= 0) & (lane < count)))
        start = start + count
        target = target + jnp.where(pos >= start, 1, 0)
    codes = codes_ref[...]
    extra = jnp.where(iota((16, rows), 0) == 0, slot + 1, 0)
    packed = dot(
        jnp.concatenate([codes, extra], 0).astype(F32).astype(BF), jnp.concatenate(places, 1)
    ).astype(BF)
    for d in range(n_y):
        cd_b[d] = packed[:, d * LANES : (d + 1) * LANES]

    pl.semaphore_wait(barrier, n_xc + n_y + n_z - 3)
    for o in range(1, n_y):
        codes_out(o).start()

    r128, l128 = iota((LANES, LANES), 0), iota((LANES, LANES), 1)
    rep = hot(iota((LANES, CODES), 0) % 16 == iota((LANES, CODES), 1) % 16)
    pick = iota((LANES, CODES), 0) % 16 == iota((LANES, CODES), 1) // 16
    fold = hot(iota((8, LANES), 1) // 16 == iota((8, LANES), 0))
    step = iota((LANES, rows), 0) % 16
    for g in range(SUB // 8):
        wide = jnp.concatenate(
            [jnp.broadcast_to(codes[g * 8 + j : g * 8 + j + 1], (16, rows)) for j in range(8)], 0
        )
        pairs = dot_nt(hot(wide // 16 == step), hot(wide % 16 == step))
        pairs = jnp.where(r128 // 16 == l128 // 16, pairs, 0.0).astype(BF)
        spread = jnp.where(pick, dot(pairs, rep), 0.0).astype(BF)
        tally = dot(fold, spread)
        for j in range(8):
            tl_v[j, g : g + 1] = tally[j : j + 1]
    for o in range(1, n_xc):
        tally1(o).start()

    for k in range(K_PARTS):
        for copy in loads[k]:
            copy.wait()
        part = dot(pooled_v[k], weight_v[k])
        if k == 0:
            res_v[...] = part
        else:
            res_v[...] += part
    acc = res_v[...]
    factor = lax.rsqrt(jnp.mean(acc * acc, axis=1, keepdims=True) + 1e-6)
    normed_v[...] = (acc * factor).astype(BF)

    group_list = target * CAP + slot
    ls_b[...] = dot(hot(iota((n_y * CAP, rows), 0) == group_list), normed_v[...]).astype(BF)
    ring(1, True).start()
    ring(1, False).start()

    xt_v[:, :rows] = normed_v[...].T
    call_v[:, :rows] = codes

    cd_r[0] = cd_b[y]
    for o in range(1, n_y):
        codes_out(o).wait_recv()
    members = jnp.zeros((CAP, LANES), F32)
    for p in range(n_y // 2):
        both = cd_r[2 * p].astype(F32) + cd_r[2 * p + 1].astype(F32)
        cols = slice(rows + p * LANES, rows + (p + 1) * LANES)
        call_v[:, cols] = both[:SUB].astype(I32)
        chosen = hot(iota((CAP, LANES), 0) + 1 == both[SUB : SUB + 1].astype(I32))
        minus = lax.dot_general(
            cent_ref[...], chosen, (((0,), (0,)), ((), ())), preferred_element_type=F32
        )
        xt_v[:, cols] = (-minus).astype(BF)
        members = members + chosen.astype(F32)
    tally_v[...] = jnp.broadcast_to(jnp.sum(members, axis=1, keepdims=True), (CAP, LANES))

    all_rows = call_v.shape[1]
    low = iota((16, all_rows), 0)

    def code_sums(o, out, kind):
        dest = lax.rem(xc + o, n_xc)
        for d in range(n_y):
            m = d * n_xc + dest
            gap = jnp.broadcast_to(call_v[pl.ds(m, 1)], (16, all_rows)) - low
            select = jnp.concatenate([hot(gap == 16 * h) for h in range(CODES // 16)], 0)
            piece = xt_v[pl.ds(pl.multiple_of(m * SUBW, SUBW), SUBW)]
            out[d * SUBW : (d + 1) * SUBW] = dot_nt(piece, select).astype(kind)

    def remote_chunk(o, carry):
        code_sums(o, s1_b.at[o], BF)
        sums1(o).start()
        return carry

    first, second = n_xc // 4 + 1, n_xc - 2
    lax.fori_loop(1, first, remote_chunk, 0)

    own = tl_v[xc]
    for o in range(1, n_xc):
        tally1(o).wait_recv()
        own = own + t1_r[o]
    for d in range(n_y):
        t2_b[d] = own[d : d + 1]
    for o in range(1, n_y):
        tally2(o).start()
    ring_step(2)
    lax.fori_loop(first, second, remote_chunk, 0)

    total = t2_b[y]
    for o in range(1, n_y):
        tally2(o).wait_recv()
        total = total + t2_r[o]
    t3_r[z] = total
    for o in range(1, n_z):
        tally3(o).start()
    ring_step(3)
    lax.fori_loop(second, n_xc, remote_chunk, 0)
    code_sums(0, own_v, F32)

    for o in range(1, n_xc):
        sums1(o).wait_recv()
    for d in range(n_y):
        part = slice(d * SUBW, (d + 1) * SUBW)
        run = own_v[part]
        for o in range(1, n_xc):
            run = run + s1_r[o, part].astype(F32)
        s2_b[d] = run
    for o in range(1, n_y):
        sums2(o).start()
    for s in range(4, far + 1):
        ring_step(s)
    run = s2_b[y]
    for o in range(1, n_y):
        sums2(o).wait_recv()
        run = run + s2_r[o]
    s3_r[z] = run.astype(BF)
    for o in range(1, n_z):
        sums3(o).start()

    lists = cent_ref[...].astype(F32) + ls_b[block(0)].astype(F32)
    for up, slots in ((True, up_r), (False, down_r)):
        ring(far, up).wait_recv()
        lists = lists + slots[far - 1].astype(F32)
    newc_ref[...] = lists * (1.0 / (1.0 + tally_v[:, :1]))

    for o in range(1, n_z):
        tally3(o).wait_recv()
    for o in range(1, n_z):
        sums3(o).wait_recv()
    total, run = t3_r[0], s3_r[0].astype(F32)
    for i in range(1, n_z):
        total = total + t3_r[i]
        run = run + s3_r[i].astype(F32)
    s4_r[xc] = run / (1.0 + total)
    for o in range(1, n_xc):
        sums4(o).start()
    for o in range(1, n_xc):
        sums4(o).wait_recv()
    book_ref[...] = s4_r[...]

    for o in range(1, n_xc):
        tally1(o).wait_send()
        sums1(o).wait_send()
        sums4(o).wait_send()
    for o in range(1, n_y):
        codes_out(o).wait_send()
        tally2(o).wait_send()
        sums2(o).wait_send()
    for s in range(1, far + 1):
        ring(s, True).wait_send()
        ring(s, False).wait_send()
    for o in range(1, n_z):
        tally3(o).wait_send()
        sums3(o).wait_send()


def local(n_z, n_xc, pooled, proj_weight, centroids, list_slot, pq_codes, route_counts):
    n_y = lax.axis_size("lists")
    rows, din = pooled.shape
    features = proj_weight.shape[1]
    all_rows = rows + n_y * CAP
    far = n_y // 2
    share = SUB // n_y
    depth = din // K_PARTS
    sem = pltpu.SemaphoreType.DMA
    vmem = pl.BlockSpec(memory_space=pltpu.VMEM)
    hbm = pl.BlockSpec(memory_space=pltpu.HBM)
    return pl.pallas_call(
        functools.partial(kernel, n_z, n_xc, n_y),
        out_shape=(
            jax.ShapeDtypeStruct(centroids.shape, F32),
            jax.ShapeDtypeStruct((share, SUBW, CODES), F32),
        ),
        in_specs=[hbm] * 6,
        out_specs=(vmem, vmem),
        scratch_shapes=[
            pltpu.SMEM((1, n_y), I32),
            pltpu.VMEM((1, rows), I32),
            pltpu.VMEM((SUB, rows), I32),
            pltpu.VMEM(centroids.shape, BF),
            pltpu.VMEM((K_PARTS, rows, depth), BF),
            pltpu.VMEM((K_PARTS, depth, features), BF),
            pltpu.VMEM((rows, features), BF),
            pltpu.VMEM((features, all_rows), BF),
            pltpu.VMEM((SUB, all_rows), I32),
            pltpu.VMEM((n_y * SUBW, CODES), F32),
            pltpu.VMEM((rows, features), F32),
            pltpu.VMEM((n_xc, n_y, CODES), F32),
            pltpu.VMEM((n_xc, n_y, CODES), F32),
            pltpu.VMEM((n_y, 1, CODES), F32),
            pltpu.VMEM((n_y, 1, CODES), F32),
            pltpu.VMEM((n_z, 1, CODES), F32),
            pltpu.VMEM((n_y, SUB + 16, LANES), BF),
            pltpu.VMEM((n_y, SUB + 16, LANES), BF),
            pltpu.VMEM((n_y * CAP, features), BF),
            pltpu.VMEM((far, CAP, features), BF),
            pltpu.VMEM((far, CAP, features), BF),
            pltpu.VMEM((CAP, LANES), F32),
            pltpu.VMEM((n_xc, n_y * SUBW, CODES), BF),
            pltpu.VMEM((n_xc, n_y * SUBW, CODES), BF),
            pltpu.VMEM((n_y, SUBW, CODES), F32),
            pltpu.VMEM((n_y, SUBW, CODES), F32),
            pltpu.VMEM((n_z, SUBW, CODES), BF),
            pltpu.VMEM((n_xc, SUBW, CODES), F32),
            sem((2, K_PARTS)), sem((4,)), sem((2, n_xc)), sem((2, n_y)), sem((2, n_z)),
            sem((2, n_y)), sem((2, far)), sem((2, far)), sem((2, n_xc)), sem((2, n_y)), sem((2, n_z)), sem((2, n_xc)),
        ],
        compiler_params=pltpu.CompilerParams(
            collective_id=0, has_side_effects=True, vmem_limit_bytes=63 << 20
        ),
        name="step",
    )(route_counts, list_slot.reshape(1, rows), pq_codes.T, centroids, pooled, proj_weight)


def solution(mesh):
    n_xc = SUB // mesh.shape["lists"]
    in_specs = (
        P(("dp", "lists"), None),
        P(),
        P(("dp", "lists"), None),
        P(("dp", "lists")),
        P(("dp", "lists"), None),
        P(("dp", "lists"), None),
    )
    out_specs = (P(("dp", "lists"), None), P("lists", None, None))
    step = functools.partial(local, mesh.shape["dp"] // n_xc, n_xc)
    return jax.shard_map(step, mesh=mesh, in_specs=in_specs, out_specs=out_specs, check_vma=False)
```

```python
import functools

import jax
import jax.numpy as jnp
from jax import lax
from jax.experimental import pallas as pl
from jax.experimental.pallas import tpu as pltpu
from jax.sharding import PartitionSpec as P

SUB = 64
CODES = 256
SUBW = 16
CAP = 64
LANES = 128
MESH = pl.DeviceIdType.MESH
BF = jnp.bfloat16
F32 = jnp.float32
I32 = jnp.int32
K_PARTS = 4
QUAD = 4


def iota(shape, dim):
    return lax.broadcasted_iota(I32, shape, dim)


def hot(mask):
    return jnp.where(mask, 1.0, 0.0).astype(BF)


def dot(a, b):
    return jnp.dot(a, b, preferred_element_type=F32)


def dot_nt(a, b):
    return lax.dot_general(a, b, (((1,), (1,)), ((), ())), preferred_element_type=F32)


def kernel(
    n_z, n_xc, n_y,
    counts_hbm, slot_hbm, codes_hbm, cent_hbm, pooled_hbm, weight_hbm,
    newc_ref, book_ref,
    counts_ref, slot_ref, codes_ref, cent_ref,
    pooled_v, weight_v, normed_v, xt_v, call_v, own_v, res_v,
    tl_v, t1_r, t2_b, t2_r,
    cd_b, cd_r, ls_b, up_r, down_r, tally_v, s1_b, s1_r, s2_b, s2_r, s3_r, s3b_r, s4_r,
    in_sem, small_sem, tl_s, t2_s, cd_s, up_s, down_s, s1_s, s2_s, s3_s, s3b_s, s4_s,
):
    rows, features = normed_v.shape[0], res_v.shape[1]
    dp, y = lax.axis_index("dp"), lax.axis_index("lists")
    z, xc = dp // n_xc, dp % n_xc

    def at_xc(o):
        return z * n_xc + lax.rem(xc + o, n_xc)

    def at_y(o):
        return lax.rem(y + o, n_y)

    n_q = n_z // QUAD
    q, r = z // QUAD, z % QUAD

    def at_q(o):
        return (lax.rem(q + o, n_q) * QUAD + r) * n_xc + xc

    def at_r(o):
        return (q * QUAD + lax.rem(r + o, QUAD)) * n_xc + xc

    def send(src, dst, sems, o, device):
        return pltpu.make_async_remote_copy(
            src_ref=src, dst_ref=dst, send_sem=sems.at[0, o], recv_sem=sems.at[1, o],
            device_id=device, device_id_type=MESH,
        )

    def tally1(o):
        return send(tl_v.at[lax.rem(xc + o, n_xc)], t1_r.at[o], tl_s, o, (at_xc(o), y))

    def tally2(o):
        return send(t2_b.at[at_y(o)], t2_r.at[o], t2_s, o, (dp, at_y(o)))

    def codes_out(o):
        return send(cd_b.at[at_y(o)], cd_r.at[o], cd_s, o, (dp, at_y(o)))

    far = n_y // 2
    half = features // 2

    def block(o):
        return pl.ds(pl.multiple_of(at_y(o) * CAP, CAP), CAP)

    def ring(s, up):
        dest = block(far + 1 - s if up else n_y - far - 1 + s)
        slots, sems = (up_r, up_s) if up else (down_r, down_s)
        src, dst = ls_b.at[dest], slots.at[s - 1]
        if s == 1:
            cols = pl.ds(0 if up else half, half)
            src, dst = src.at[:, cols], dst.at[:, cols]
        return send(src, dst, sems, s - 1, (dp, at_y(1 if up else n_y - 1)))

    def ring_step(s):
        for up in (True, False):
            ring(s - 1, up).wait_recv()
            dest = block(far + 1 - s if up else n_y - far - 1 + s)
            cols = slice(0, features)
            if s == 2:
                cols = slice(0, half) if up else slice(half, features)
            came = (up_r if up else down_r)[s - 2, :, cols].astype(F32)
            ls_b[dest, cols] = (ls_b[dest, cols].astype(F32) + came).astype(BF)
            ring(s, up).start()

    def sums1(o):
        return send(s1_b.at[o], s1_r.at[o], s1_s, o, (at_xc(o), y))

    def sums2(o):
        return send(s2_b.at[at_y(o)], s2_r.at[o], s2_s, o, (dp, at_y(o)))

    def sums3(o):
        return send(s3_r.at[q], s3_r.at[q], s3_s, o, (at_q(o), y))

    def sums3b(o):
        return send(s3b_r.at[r], s3b_r.at[r], s3b_s, o, (at_r(o), y))

    def sums4(o):
        return send(s4_r.at[xc], s4_r.at[xc], s4_s, o, (at_xc(o), y))

    small = [
        pltpu.make_async_copy(src, dst, small_sem.at[i])
        for i, (src, dst) in enumerate(
            (
                (counts_hbm, counts_ref),
                (slot_hbm, slot_ref),
                (codes_hbm, codes_ref),
                (cent_hbm, cent_ref),
            )
        )
    ]
    for copy in small:
        copy.start()
    depth = weight_v.shape[1]
    loads = []
    for k in range(K_PARTS):
        cols = pl.ds(k * depth, depth)
        pair = (
            pltpu.make_async_copy(pooled_hbm.at[:, cols], pooled_v.at[k], in_sem.at[0, k]),
            pltpu.make_async_copy(weight_hbm.at[cols], weight_v.at[k], in_sem.at[1, k]),
        )
        for copy in pair:
            copy.start()
        loads.append(pair)

    barrier = pltpu.get_barrier_semaphore()
    for o in range(1, n_xc):
        pl.semaphore_signal(barrier, inc=1, device_id=(at_xc(o), y), device_id_type=MESH)
    for o in range(1, n_y):
        pl.semaphore_signal(barrier, inc=1, device_id=(dp, at_y(o)), device_id_type=MESH)
    for o in range(1, n_q):
        pl.semaphore_signal(barrier, inc=1, device_id=(at_q(o), y), device_id_type=MESH)
    for o in range(1, QUAD):
        pl.semaphore_signal(barrier, inc=1, device_id=(at_r(o), y), device_id_type=MESH)

    for copy in small:
        copy.wait()
    slot = slot_ref[...]
    pos = iota((1, rows), 1)
    target = jnp.zeros((1, rows), I32)
    lane = iota((rows, LANES), 1) - (y % 2) * CAP
    row = iota((rows, LANES), 0)
    start = 0
    places = []
    for d in range(n_y):
        count = counts_ref[0, d]
        places.append(hot((row == lane + start) & (lane >= 0) & (lane < count)))
        start = start + count
        target = target + jnp.where(pos >= start, 1, 0)
    codes = codes_ref[...]
    extra = jnp.where(iota((16, rows), 0) == 0, slot + 1, 0)
    packed = dot(
        jnp.concatenate([codes, extra], 0).astype(F32).astype(BF), jnp.concatenate(places, 1)
    ).astype(BF)
    for d in range(n_y):
        cd_b[d] = packed[:, d * LANES : (d + 1) * LANES]

    pl.semaphore_wait(barrier, n_xc + n_y + n_q + QUAD - 4)
    for o in range(1, n_y):
        codes_out(o).start()

    r128, l128 = iota((LANES, LANES), 0), iota((LANES, LANES), 1)
    rep = hot(iota((LANES, CODES), 0) % 16 == iota((LANES, CODES), 1) % 16)
    pick = iota((LANES, CODES), 0) % 16 == iota((LANES, CODES), 1) // 16
    fold = hot(iota((8, LANES), 1) // 16 == iota((8, LANES), 0))
    step = iota((LANES, rows), 0) % 16
    for g in range(SUB // 8):
        wide = jnp.concatenate(
            [jnp.broadcast_to(codes[g * 8 + j : g * 8 + j + 1], (16, rows)) for j in range(8)], 0
        )
        pairs = dot_nt(hot(wide // 16 == step), hot(wide % 16 == step))
        pairs = jnp.where(r128 // 16 == l128 // 16, pairs, 0.0).astype(BF)
        spread = jnp.where(pick, dot(pairs, rep), 0.0).astype(BF)
        tally = dot(fold, spread)
        for j in range(8):
            tl_v[j, g : g + 1] = tally[j : j + 1]
    for o in range(1, n_xc):
        tally1(o).start()

    for k in range(K_PARTS):
        for copy in loads[k]:
            copy.wait()
        part = dot(pooled_v[k], weight_v[k])
        if k == 0:
            res_v[...] = part
        else:
            res_v[...] += part
    acc = res_v[...]
    factor = lax.rsqrt(jnp.mean(acc * acc, axis=1, keepdims=True) + 1e-6)
    normed_v[...] = (acc * factor).astype(BF)

    group_list = target * CAP + slot
    ls_b[...] = dot(hot(iota((n_y * CAP, rows), 0) == group_list), normed_v[...]).astype(BF)
    ring(1, True).start()
    ring(1, False).start()

    xt_v[:, :rows] = normed_v[...].T
    call_v[:, :rows] = codes

    cd_r[0] = cd_b[y]
    for o in range(1, n_y):
        codes_out(o).wait_recv()
    members = jnp.zeros((CAP, LANES), F32)
    for p in range(n_y // 2):
        both = cd_r[2 * p].astype(F32) + cd_r[2 * p + 1].astype(F32)
        cols = slice(rows + p * LANES, rows + (p + 1) * LANES)
        call_v[:, cols] = both[:SUB].astype(I32)
        chosen = hot(iota((CAP, LANES), 0) + 1 == both[SUB : SUB + 1].astype(I32))
        minus = lax.dot_general(
            cent_ref[...], chosen, (((0,), (0,)), ((), ())), preferred_element_type=F32
        )
        xt_v[:, cols] = (-minus).astype(BF)
        members = members + chosen.astype(F32)
    tally_v[...] = jnp.broadcast_to(jnp.sum(members, axis=1, keepdims=True), (CAP, LANES))

    all_rows = call_v.shape[1]
    low = iota((16, all_rows), 0)

    def code_sums(o, out, kind):
        dest = lax.rem(xc + o, n_xc)
        for d in range(n_y):
            m = d * n_xc + dest
            gap = jnp.broadcast_to(call_v[pl.ds(m, 1)], (16, all_rows)) - low
            select = jnp.concatenate([hot(gap == 16 * h) for h in range(CODES // 16)], 0)
            piece = xt_v[pl.ds(pl.multiple_of(m * SUBW, SUBW), SUBW)]
            out[d * SUBW : (d + 1) * SUBW] = dot_nt(piece, select).astype(kind)

    def remote_chunk(o, carry):
        code_sums(o, s1_b.at[o], BF)
        sums1(o).start()
        return carry

    first, second = n_xc // 4 + 1, n_xc - 2
    lax.fori_loop(1, first, remote_chunk, 0)

    own = tl_v[xc]
    for o in range(1, n_xc):
        tally1(o).wait_recv()
        own = own + t1_r[o]
    for d in range(n_y):
        t2_b[d] = own[d : d + 1]
    for o in range(1, n_y):
        tally2(o).start()
    ring_step(2)
    lax.fori_loop(first, second, remote_chunk, 0)

    ring_step(3)
    lax.fori_loop(second, n_xc, remote_chunk, 0)
    code_sums(0, own_v, F32)

    for o in range(1, n_xc):
        sums1(o).wait_recv()
    for d in range(n_y):
        part = slice(d * SUBW, (d + 1) * SUBW)
        run = own_v[part]
        for o in range(1, n_xc):
            run = run + s1_r[o, part].astype(F32)
        s2_b[d] = run
    for o in range(1, n_y):
        sums2(o).start()
    total = t2_b[y]
    for o in range(1, n_y):
        tally2(o).wait_recv()
        total = total + t2_r[o]
    run = s2_b[y]
    for o in range(1, n_y):
        sums2(o).wait_recv()
        run = run + s2_r[o]
    s3_r[q, :SUBW] = run
    s3_r[q, SUBW:] = jnp.broadcast_to(total, (8, CODES))
    for o in range(1, n_q):
        sums3(o).start()
    for s in range(4, far + 1):
        ring_step(s)
    for o in range(1, n_q):
        sums3(o).wait_recv()
    run = s3_r[0]
    for i in range(1, n_q):
        run = run + s3_r[i]
    s3b_r[r] = run
    for o in range(1, QUAD):
        sums3b(o).start()
    for o in range(1, QUAD):
        sums3b(o).wait_recv()
    run = s3b_r[0]
    for i in range(1, QUAD):
        run = run + s3b_r[i]
    s4_r[xc] = run[:SUBW] / (1.0 + run[SUBW : SUBW + 1])
    for o in range(1, n_xc):
        sums4(o).start()

    lists = cent_ref[...].astype(F32) + ls_b[block(0)].astype(F32)
    for up, slots in ((True, up_r), (False, down_r)):
        ring(far, up).wait_recv()
        lists = lists + slots[far - 1].astype(F32)
    newc_ref[...] = lists * (1.0 / (1.0 + tally_v[:, :1]))

    for o in range(1, n_xc):
        sums4(o).wait_recv()
    book_ref[...] = s4_r[...]

    for o in range(1, n_xc):
        tally1(o).wait_send()
        sums1(o).wait_send()
        sums4(o).wait_send()
    for o in range(1, n_y):
        codes_out(o).wait_send()
        tally2(o).wait_send()
        sums2(o).wait_send()
    for s in range(1, far + 1):
        ring(s, True).wait_send()
        ring(s, False).wait_send()
    for o in range(1, n_q):
        sums3(o).wait_send()
    for o in range(1, QUAD):
        sums3b(o).wait_send()


def local(n_z, n_xc, pooled, proj_weight, centroids, list_slot, pq_codes, route_counts):
    n_y = lax.axis_size("lists")
    rows, din = pooled.shape
    features = proj_weight.shape[1]
    all_rows = rows + n_y * CAP
    far = n_y // 2
    share = SUB // n_y
    depth = din // K_PARTS
    sem = pltpu.SemaphoreType.DMA
    slots = list_slot.reshape(1, rows)
    operands = (route_counts, slots, pq_codes.T, centroids, pooled, proj_weight)
    vmem = pl.BlockSpec(memory_space=pltpu.VMEM)
    hbm = pl.BlockSpec(memory_space=pltpu.HBM)
    return pl.pallas_call(
        functools.partial(kernel, n_z, n_xc, n_y),
        out_shape=(
            jax.ShapeDtypeStruct(centroids.shape, F32),
            jax.ShapeDtypeStruct((share, SUBW, CODES), F32),
        ),
        in_specs=[hbm] * 6,
        out_specs=(vmem, vmem),
        scratch_shapes=[
            pltpu.SMEM((1, n_y), I32),
            pltpu.VMEM((1, rows), I32),
            pltpu.VMEM((SUB, rows), I32),
            pltpu.VMEM(centroids.shape, BF),
            pltpu.VMEM((K_PARTS, rows, depth), BF),
            pltpu.VMEM((K_PARTS, depth, features), BF),
            pltpu.VMEM((rows, features), BF),
            pltpu.VMEM((features, all_rows), BF),
            pltpu.VMEM((SUB, all_rows), I32),
            pltpu.VMEM((n_y * SUBW, CODES), F32),
            pltpu.VMEM((rows, features), F32),
            pltpu.VMEM((n_xc, n_y, CODES), F32),
            pltpu.VMEM((n_xc, n_y, CODES), F32),
            pltpu.VMEM((n_y, 1, CODES), F32),
            pltpu.VMEM((n_y, 1, CODES), F32),
            pltpu.VMEM((n_y, SUB + 16, LANES), BF),
            pltpu.VMEM((n_y, SUB + 16, LANES), BF),
            pltpu.VMEM((n_y * CAP, features), BF),
            pltpu.VMEM((far, CAP, features), BF),
            pltpu.VMEM((far, CAP, features), BF),
            pltpu.VMEM((CAP, LANES), F32),
            pltpu.VMEM((n_xc, n_y * SUBW, CODES), BF),
            pltpu.VMEM((n_xc, n_y * SUBW, CODES), BF),
            pltpu.VMEM((n_y, SUBW, CODES), F32),
            pltpu.VMEM((n_y, SUBW, CODES), F32),
            pltpu.VMEM((n_z // QUAD, SUBW + 8, CODES), F32),
            pltpu.VMEM((QUAD, SUBW + 8, CODES), F32),
            pltpu.VMEM((n_xc, SUBW, CODES), F32),
            sem((2, K_PARTS)), sem((4,)), sem((2, n_xc)), sem((2, n_y)), sem((2, n_y)),
            sem((2, far)), sem((2, far)), sem((2, n_xc)), sem((2, n_y)),
            sem((2, n_z // QUAD)), sem((2, QUAD)), sem((2, n_xc)),
        ],
        compiler_params=pltpu.CompilerParams(
            collective_id=0, has_side_effects=True, vmem_limit_bytes=48 << 20
        ),
        name="step",
    )(*(pltpu.with_memory_space_constraint(v, pltpu.HBM) for v in operands))


def solution(mesh):
    n_xc = SUB // mesh.shape["lists"]
    in_specs = (
        P(("dp", "lists"), None),
        P(),
        P(("dp", "lists"), None),
        P(("dp", "lists")),
        P(("dp", "lists"), None),
        P(("dp", "lists"), None),
    )
    out_specs = (P(("dp", "lists"), None), P("lists", None, None))
    step = functools.partial(local, mesh.shape["dp"] // n_xc, n_xc)
    return jax.shard_map(step, mesh=mesh, in_specs=in_specs, out_specs=out_specs, check_vma=False)
```

```python
import functools

import jax
import jax.numpy as jnp
from jax import lax
from jax.experimental import pallas as pl
from jax.experimental.pallas import tpu as pltpu
from jax.sharding import PartitionSpec as P

SUB = 64
CODES = 256
SUBW = 16
CAP = 64
LANES = 128
MESH = pl.DeviceIdType.MESH
BF = jnp.bfloat16
F32 = jnp.float32
I32 = jnp.int32
K_PARTS = 4


def iota(shape, dim):
    return lax.broadcasted_iota(I32, shape, dim)


def hot(mask):
    return jnp.where(mask, 1.0, 0.0).astype(BF)


def dot(a, b):
    return jnp.dot(a, b, preferred_element_type=F32)


def dot_nt(a, b):
    return lax.dot_general(a, b, (((1,), (1,)), ((), ())), preferred_element_type=F32)


def kernel(
    n_z, n_xc, n_y,
    counts_hbm, slot_hbm, codes_hbm, cent_hbm, pooled_hbm, weight_hbm,
    newc_ref, book_ref,
    counts_ref, slot_ref, codes_ref, cent_ref,
    pooled_v, weight_v, normed_v, xt_v, call_v, own_v, res_v,
    tl_v, t1_r, t2_b, t2_r, t3_r,
    cd_b, cd_r, centt_v, ls_b, up_r, down_r, tally_v, s1_b, s1_r, s2_b, s2_r, s3_r, s4_r,
    in_sem, small_sem, tl_s, t2_s, t3_s, cd_s, up_s, down_s, s1_s, s2_s, s3_s, s4_s,
):
    rows, features = normed_v.shape[0], res_v.shape[1]
    dp, y = lax.axis_index("dp"), lax.axis_index("lists")
    z, xc = dp // n_xc, dp % n_xc

    def at_xc(o):
        return z * n_xc + lax.rem(xc + o, n_xc)

    def at_y(o):
        return lax.rem(y + o, n_y)

    def at_z(o):
        return lax.rem(z + o, n_z) * n_xc + xc

    def send(src, dst, sems, o, device):
        return pltpu.make_async_remote_copy(
            src_ref=src, dst_ref=dst, send_sem=sems.at[0, o], recv_sem=sems.at[1, o],
            device_id=device, device_id_type=MESH,
        )

    def tally1(o):
        return send(tl_v.at[lax.rem(xc + o, n_xc)], t1_r.at[o], tl_s, o, (at_xc(o), y))

    def tally2(o):
        return send(t2_b.at[at_y(o)], t2_r.at[o], t2_s, o, (dp, at_y(o)))

    def codes_out(o):
        return send(cd_b.at[at_y(o)], cd_r.at[o], cd_s, o, (dp, at_y(o)))

    far = n_y // 2
    half = features // 2

    def block(o):
        return pl.ds(pl.multiple_of(at_y(o) * CAP, CAP), CAP)

    def ring(s, up):
        dest = block(far + 1 - s if up else n_y - far - 1 + s)
        slots, sems = (up_r, up_s) if up else (down_r, down_s)
        src, dst = ls_b.at[dest], slots.at[s - 1]
        if s == 1:
            cols = pl.ds(0 if up else half, half)
            src, dst = src.at[:, cols], dst.at[:, cols]
        return send(src, dst, sems, s - 1, (dp, at_y(1 if up else n_y - 1)))

    def ring_step(s):
        for up in (True, False):
            ring(s - 1, up).wait_recv()
            dest = block(far + 1 - s if up else n_y - far - 1 + s)
            cols = slice(0, features)
            if s == 2:
                cols = slice(0, half) if up else slice(half, features)
            came = (up_r if up else down_r)[s - 2, :, cols].astype(F32)
            ls_b[dest, cols] = (ls_b[dest, cols].astype(F32) + came).astype(BF)
            ring(s, up).start()

    def sums1(o):
        return send(s1_b.at[o], s1_r.at[o], s1_s, o, (at_xc(o), y))

    def sums2(o):
        return send(s2_b.at[at_y(o)], s2_r.at[o], s2_s, o, (dp, at_y(o)))

    def tally3(o):
        return send(t3_r.at[z], t3_r.at[z], t3_s, o, (at_z(o), y))

    def sums3(o):
        return send(s3_r.at[z], s3_r.at[z], s3_s, o, (at_z(o), y))

    def sums4(o):
        return send(s4_r.at[xc], s4_r.at[xc], s4_s, o, (at_xc(o), y))

    small = [
        pltpu.make_async_copy(src, dst, small_sem.at[i])
        for i, (src, dst) in enumerate(
            (
                (counts_hbm, counts_ref),
                (slot_hbm, slot_ref),
                (codes_hbm, codes_ref),
                (cent_hbm, cent_ref),
            )
        )
    ]
    for copy in small:
        copy.start()
    depth = weight_v.shape[1]
    loads = []
    for k in range(K_PARTS):
        cols = pl.ds(k * depth, depth)
        pair = (
            pltpu.make_async_copy(pooled_hbm.at[:, cols], pooled_v.at[k], in_sem.at[0, k]),
            pltpu.make_async_copy(weight_hbm.at[cols], weight_v.at[k], in_sem.at[1, k]),
        )
        for copy in pair:
            copy.start()
        loads.append(pair)

    barrier = pltpu.get_barrier_semaphore()
    for o in range(1, n_xc):
        pl.semaphore_signal(barrier, inc=1, device_id=(at_xc(o), y), device_id_type=MESH)
    for o in range(1, n_y):
        pl.semaphore_signal(barrier, inc=1, device_id=(dp, at_y(o)), device_id_type=MESH)
    for o in range(1, n_z):
        pl.semaphore_signal(barrier, inc=1, device_id=(at_z(o), y), device_id_type=MESH)

    for copy in small:
        copy.wait()
    slot = slot_ref[...]
    pos = iota((1, rows), 1)
    target = jnp.zeros((1, rows), I32)
    row = iota((2 * rows, LANES), 0)
    lane = iota((2 * rows, LANES), 1) - row // rows * CAP
    row = row % rows
    start = 0
    places = []
    for d in range(n_y):
        count = counts_ref[0, d]
        places.append(hot((row == lane + start) & (lane >= 0) & (lane < count)))
        start = start + count
        target = target + jnp.where(pos >= start, 1, 0)
    codes = codes_ref[...]
    codes_half = SUB // 2
    extra = jnp.where(iota((16, rows), 0) == 0, slot + 1, 0)
    halves = jnp.concatenate(
        [
            jnp.concatenate([codes[:codes_half], extra], 0),
            jnp.concatenate([codes[codes_half:], jnp.zeros((16, rows), I32)], 0),
        ],
        1,
    )
    packed = dot(halves.astype(F32).astype(BF), jnp.concatenate(places, 1)).astype(BF)
    for d in range(n_y):
        cd_b[d] = packed[:, d * LANES : (d + 1) * LANES]

    pl.semaphore_wait(barrier, n_xc + n_y + n_z - 3)
    for o in range(1, n_y):
        codes_out(o).start()

    centt_v[...] = (-cent_ref[...].astype(F32)).T.astype(BF)

    r128, l128 = iota((LANES, LANES), 0), iota((LANES, LANES), 1)
    rep = hot(iota((LANES, CODES), 0) % 16 == iota((LANES, CODES), 1) % 16)
    pick = iota((LANES, CODES), 0) % 16 == iota((LANES, CODES), 1) // 16
    fold = hot(iota((8, LANES), 1) // 16 == iota((8, LANES), 0))
    step = iota((LANES, rows), 0) % 16
    for g in range(SUB // 8):
        wide = jnp.concatenate(
            [jnp.broadcast_to(codes[g * 8 + j : g * 8 + j + 1], (16, rows)) for j in range(8)], 0
        )
        pairs = dot_nt(hot(wide // 16 == step), hot(wide % 16 == step))
        pairs = jnp.where(r128 // 16 == l128 // 16, pairs, 0.0).astype(BF)
        spread = jnp.where(pick, dot(pairs, rep), 0.0).astype(BF)
        tally = dot(fold, spread)
        for j in range(8):
            tl_v[j, g : g + 1] = tally[j : j + 1]
    for o in range(1, n_xc):
        tally1(o).start()

    for k in range(K_PARTS):
        for copy in loads[k]:
            copy.wait()
        part = dot(pooled_v[k], weight_v[k])
        if k == 0:
            res_v[...] = part
        else:
            res_v[...] += part
    acc = res_v[...]
    factor = lax.rsqrt(jnp.mean(acc * acc, axis=1, keepdims=True) + 1e-6)
    normed_v[...] = (acc * factor).astype(BF)

    group_list = target * CAP + slot
    ls_b[...] = dot(hot(iota((n_y * CAP, rows), 0) == group_list), normed_v[...]).astype(BF)
    ring(1, True).start()
    ring(1, False).start()

    xt_v[:, :rows] = normed_v[...].T
    call_v[:, :rows] = codes

    cd_r[0] = cd_b[y]
    for o in range(1, n_y):
        codes_out(o).wait_recv()
    low_lanes = iota((codes_half + 16, LANES), 1) < CAP
    picks = []
    members = jnp.zeros((CAP, LANES), F32)
    for p in range(n_y // 2):
        left, right = cd_r[2 * p].astype(F32), cd_r[2 * p + 1].astype(F32)
        upper = jnp.where(low_lanes, left, pltpu.roll(right, CAP, 1))
        lower = jnp.where(low_lanes, pltpu.roll(left, CAP, 1), right)
        cols = slice(rows + p * LANES, rows + (p + 1) * LANES)
        call_v[:codes_half, cols] = upper[:codes_half].astype(I32)
        call_v[codes_half:, cols] = lower[:codes_half].astype(I32)
        chosen = hot(iota((CAP, LANES), 0) + 1 == upper[codes_half : codes_half + 1].astype(I32))
        picks.append(chosen)
        members = members + chosen.astype(F32)
    xt_v[:, rows:] = dot(centt_v[...], jnp.concatenate(picks, 1)).astype(BF)
    tally_v[...] = jnp.broadcast_to(jnp.sum(members, axis=1, keepdims=True), (CAP, LANES))

    all_rows = call_v.shape[1]
    low = iota((16, all_rows), 0)

    def code_sums(o, out, kind):
        dest = lax.rem(xc + o, n_xc)
        for d in range(n_y):
            m = d * n_xc + dest
            gap = jnp.broadcast_to(call_v[pl.ds(m, 1)], (16, all_rows)) - low
            select = jnp.concatenate([hot(gap == 16 * h) for h in range(CODES // 16)], 0)
            piece = xt_v[pl.ds(pl.multiple_of(m * SUBW, SUBW), SUBW)]
            out[d * SUBW : (d + 1) * SUBW] = dot_nt(piece, select).astype(kind)

    def remote_chunk(o, carry):
        code_sums(o, s1_b.at[o], BF)
        sums1(o).start()
        return carry

    first, second = 2, n_xc - 2
    lax.fori_loop(1, first, remote_chunk, 0)

    own = tl_v[xc]
    for o in range(1, n_xc):
        tally1(o).wait_recv()
        own = own + t1_r[o]
    for d in range(n_y):
        t2_b[d] = own[d : d + 1]
    for o in range(1, n_y):
        tally2(o).start()
    ring_step(2)
    lax.fori_loop(first, second, remote_chunk, 0)

    ring_step(3)
    lax.fori_loop(second, n_xc, remote_chunk, 0)
    code_sums(0, own_v, F32)

    for o in range(1, n_xc):
        sums1(o).wait_recv()
    for d in range(n_y):
        part = slice(d * SUBW, (d + 1) * SUBW)
        run = own_v[part]
        for o in range(1, n_xc):
            run = run + s1_r[o, part].astype(F32)
        s2_b[d] = run
    for o in range(1, n_y):
        sums2(o).start()
    total = t2_b[y]
    for o in range(1, n_y):
        tally2(o).wait_recv()
        total = total + t2_r[o]
    t3_r[z] = total
    for o in range(1, n_z):
        tally3(o).start()
    run = s2_b[y]
    for o in range(1, n_y):
        sums2(o).wait_recv()
        run = run + s2_r[o]
    s3_r[z] = run.astype(BF)
    for o in range(1, n_z):
        sums3(o).start()
    for s in range(4, far + 1):
        ring_step(s)
    for o in range(1, n_z):
        tally3(o).wait_recv()
    for o in range(1, n_z):
        sums3(o).wait_recv()
    total, run = t3_r[0], s3_r[0].astype(F32)
    for i in range(1, n_z):
        total = total + t3_r[i]
        run = run + s3_r[i].astype(F32)
    s4_r[xc] = run / (1.0 + total)
    for o in range(1, n_xc):
        sums4(o).start()

    lists = cent_ref[...].astype(F32) + ls_b[block(0)].astype(F32)
    for up, slots in ((True, up_r), (False, down_r)):
        ring(far, up).wait_recv()
        lists = lists + slots[far - 1].astype(F32)
    newc_ref[...] = lists * (1.0 / (1.0 + tally_v[:, :1]))

    for o in range(1, n_xc):
        sums4(o).wait_recv()
    book_ref[...] = s4_r[...]

    for o in range(1, n_xc):
        tally1(o).wait_send()
        sums1(o).wait_send()
        sums4(o).wait_send()
    for o in range(1, n_y):
        codes_out(o).wait_send()
        tally2(o).wait_send()
        sums2(o).wait_send()
    for s in range(1, far + 1):
        ring(s, True).wait_send()
        ring(s, False).wait_send()
    for o in range(1, n_z):
        tally3(o).wait_send()
        sums3(o).wait_send()


def local(n_z, n_xc, pooled, proj_weight, centroids, list_slot, pq_codes, route_counts):
    n_y = lax.axis_size("lists")
    rows, din = pooled.shape
    features = proj_weight.shape[1]
    all_rows = rows + n_y * CAP
    far = n_y // 2
    share = SUB // n_y
    depth = din // K_PARTS
    sem = pltpu.SemaphoreType.DMA
    slots = list_slot.reshape(1, rows)
    operands = (route_counts, slots, pq_codes.T, centroids, pooled, proj_weight)
    vmem = pl.BlockSpec(memory_space=pltpu.VMEM)
    hbm = pl.BlockSpec(memory_space=pltpu.HBM)
    return pl.pallas_call(
        functools.partial(kernel, n_z, n_xc, n_y),
        out_shape=(
            jax.ShapeDtypeStruct(centroids.shape, F32),
            jax.ShapeDtypeStruct((share, SUBW, CODES), F32),
        ),
        in_specs=[hbm] * 6,
        out_specs=(vmem, vmem),
        scratch_shapes=[
            pltpu.SMEM((1, n_y), I32),
            pltpu.VMEM((1, rows), I32),
            pltpu.VMEM((SUB, rows), I32),
            pltpu.VMEM(centroids.shape, BF),
            pltpu.VMEM((K_PARTS, rows, depth), BF),
            pltpu.VMEM((K_PARTS, depth, features), BF),
            pltpu.VMEM((rows, features), BF),
            pltpu.VMEM((features, all_rows), BF),
            pltpu.VMEM((SUB, all_rows), I32),
            pltpu.VMEM((n_y * SUBW, CODES), F32),
            pltpu.VMEM((rows, features), F32),
            pltpu.VMEM((n_xc, n_y, CODES), F32),
            pltpu.VMEM((n_xc, n_y, CODES), F32),
            pltpu.VMEM((n_y, 1, CODES), F32),
            pltpu.VMEM((n_y, 1, CODES), F32),
            pltpu.VMEM((n_z, 1, CODES), F32),
            pltpu.VMEM((n_y, SUB // 2 + 16, LANES), BF),
            pltpu.VMEM((n_y, SUB // 2 + 16, LANES), BF),
            pltpu.VMEM((features, CAP), BF),
            pltpu.VMEM((n_y * CAP, features), BF),
            pltpu.VMEM((far, CAP, features), BF),
            pltpu.VMEM((far, CAP, features), BF),
            pltpu.VMEM((CAP, LANES), F32),
            pltpu.VMEM((n_xc, n_y * SUBW, CODES), BF),
            pltpu.VMEM((n_xc, n_y * SUBW, CODES), BF),
            pltpu.VMEM((n_y, SUBW, CODES), F32),
            pltpu.VMEM((n_y, SUBW, CODES), F32),
            pltpu.VMEM((n_z, SUBW, CODES), BF),
            pltpu.VMEM((n_xc, SUBW, CODES), F32),
            sem((2, K_PARTS)), sem((4,)), sem((2, n_xc)), sem((2, n_y)), sem((2, n_z)), sem((2, n_y)),
            sem((2, far)), sem((2, far)), sem((2, n_xc)), sem((2, n_y)),
            sem((2, n_z)), sem((2, n_xc)),
        ],
        compiler_params=pltpu.CompilerParams(
            collective_id=0, has_side_effects=True, vmem_limit_bytes=48 << 20
        ),
        name="step",
    )(*(pltpu.with_memory_space_constraint(v, pltpu.HBM) for v in operands))


def solution(mesh):
    n_xc = SUB // mesh.shape["lists"]
    in_specs = (
        P(("dp", "lists"), None),
        P(),
        P(("dp", "lists"), None),
        P(("dp", "lists")),
        P(("dp", "lists"), None),
        P(("dp", "lists"), None),
    )
    out_specs = (P(("dp", "lists"), None), P("lists", None, None))
    step = functools.partial(local, mesh.shape["dp"] // n_xc, n_xc)
    return jax.shard_map(step, mesh=mesh, in_specs=in_specs, out_specs=out_specs, check_vma=False)
```

```python
import functools

import jax
import jax.numpy as jnp
from jax import lax
from jax.experimental import pallas as pl
from jax.experimental.pallas import tpu as pltpu
from jax.sharding import PartitionSpec as P

SUB = 64
CODES = 256
SUBW = 16
CAP = 64
LANES = 128
MESH = pl.DeviceIdType.MESH
BF = jnp.bfloat16
F32 = jnp.float32
I32 = jnp.int32
K_PARTS = 4


def iota(shape, dim):
    return lax.broadcasted_iota(I32, shape, dim)


def hot(mask):
    return jnp.where(mask, 1.0, 0.0).astype(BF)


def dot(a, b):
    return jnp.dot(a, b, preferred_element_type=F32)


def dot_nt(a, b):
    return lax.dot_general(a, b, (((1,), (1,)), ((), ())), preferred_element_type=F32)


def far_first(n):
    return sorted(range(1, n), key=lambda o: -min(o, n - o))


def kernel(
    n_z, n_xc, n_y,
    counts_hbm, slot_hbm, codes_hbm, cent_hbm, pooled_hbm, weight_hbm,
    newc_ref, book_ref,
    counts_ref, slot_ref, codes_ref, cent_ref,
    pooled_v, weight_v, normed_v, xt_v, call_v, own_v, res_v,
    tl_v, t1_r, t2_b, t2_r, t3_r,
    cd_b, cd_r, centt_v, ls_b, up_r, down_r, tally_v, s1_b, s1_r, s2_b, s2_r, s3_r, s4_r,
    in_sem, small_sem, tl_s, t2_s, t3_s, cd_s, up_s, down_s, s1_s, s2_s, s3_s, s4_s,
):
    rows, features = normed_v.shape[0], res_v.shape[1]
    dp, y = lax.axis_index("dp"), lax.axis_index("lists")
    z, xc = dp // n_xc, dp % n_xc

    def at_xc(o):
        return z * n_xc + lax.rem(xc + o, n_xc)

    def at_y(o):
        return lax.rem(y + o, n_y)

    def at_z(o):
        return lax.rem(z + o, n_z) * n_xc + xc

    def send(src, dst, sems, o, device):
        return pltpu.make_async_remote_copy(
            src_ref=src, dst_ref=dst, send_sem=sems.at[0, o], recv_sem=sems.at[1, o],
            device_id=device, device_id_type=MESH,
        )

    def tally1(o):
        return send(tl_v.at[lax.rem(xc + o, n_xc)], t1_r.at[o], tl_s, o, (at_xc(o), y))

    def tally2(o):
        return send(t2_b.at[at_y(o)], t2_r.at[o], t2_s, o, (dp, at_y(o)))

    def codes_out(o):
        return send(cd_b.at[at_y(o)], cd_r.at[o], cd_s, o, (dp, at_y(o)))

    far = n_y // 2
    half = features // 2

    def block(o):
        return pl.ds(pl.multiple_of(at_y(o) * CAP, CAP), CAP)

    def ring(s, up):
        dest = block(far + 1 - s if up else n_y - far - 1 + s)
        slots, sems = (up_r, up_s) if up else (down_r, down_s)
        src, dst = ls_b.at[dest], slots.at[s - 1]
        if s == 1:
            cols = pl.ds(0 if up else half, half)
            src, dst = src.at[:, cols], dst.at[:, cols]
        return send(src, dst, sems, s - 1, (dp, at_y(1 if up else n_y - 1)))

    def ring_step(s):
        for up in (True, False):
            ring(s - 1, up).wait_recv()
            dest = block(far + 1 - s if up else n_y - far - 1 + s)
            cols = slice(0, features)
            if s == 2:
                cols = slice(0, half) if up else slice(half, features)
            came = (up_r if up else down_r)[s - 2, :, cols].astype(F32)
            ls_b[dest, cols] = (ls_b[dest, cols].astype(F32) + came).astype(BF)
            ring(s, up).start()

    def sums1(o):
        return send(s1_b.at[o], s1_r.at[o], s1_s, o, (at_xc(o), y))

    def sums2(o):
        return send(s2_b.at[at_y(o)], s2_r.at[o], s2_s, o, (dp, at_y(o)))

    def tally3(o):
        return send(t3_r.at[z], t3_r.at[z], t3_s, o, (at_z(o), y))

    def sums3(o):
        return send(s3_r.at[z], s3_r.at[z], s3_s, o, (at_z(o), y))

    def sums4(o):
        return send(s4_r.at[xc], s4_r.at[xc], s4_s, o, (at_xc(o), y))

    barrier = pltpu.get_barrier_semaphore()
    for o in far_first(n_y):
        pl.semaphore_signal(barrier, inc=1, device_id=(dp, at_y(o)), device_id_type=MESH)
    for o in far_first(n_xc):
        pl.semaphore_signal(barrier, inc=1, device_id=(at_xc(o), y), device_id_type=MESH)
    for o in range(1, n_z):
        pl.semaphore_signal(barrier, inc=1, device_id=(at_z(o), y), device_id_type=MESH)

    small = [
        pltpu.make_async_copy(src, dst, small_sem.at[i])
        for i, (src, dst) in enumerate(
            (
                (counts_hbm, counts_ref),
                (slot_hbm, slot_ref),
                (codes_hbm, codes_ref),
                (cent_hbm, cent_ref),
            )
        )
    ]
    for copy in small:
        copy.start()
    depth = weight_v.shape[1]
    loads = []
    for k in range(K_PARTS):
        cols = pl.ds(k * depth, depth)
        pair = (
            pltpu.make_async_copy(pooled_hbm.at[:, cols], pooled_v.at[k], in_sem.at[0, k]),
            pltpu.make_async_copy(weight_hbm.at[cols], weight_v.at[k], in_sem.at[1, k]),
        )
        for copy in pair:
            copy.start()
        loads.append(pair)

    for copy in small:
        copy.wait()
    slot = slot_ref[...]
    pos = iota((1, rows), 1)
    target = jnp.zeros((1, rows), I32)
    row = iota((2 * rows, LANES), 0)
    lane = iota((2 * rows, LANES), 1) - row // rows * CAP
    row = row % rows
    start = 0
    places = []
    for d in range(n_y):
        count = counts_ref[0, d]
        places.append(hot((row == lane + start) & (lane >= 0) & (lane < count)))
        start = start + count
        target = target + jnp.where(pos >= start, 1, 0)
    codes = codes_ref[...]
    codes_half = SUB // 2
    extra = jnp.where(iota((16, rows), 0) == 0, slot + 1, 0)
    halves = jnp.concatenate(
        [
            jnp.concatenate([codes[:codes_half], extra], 0),
            jnp.concatenate([codes[codes_half:], jnp.zeros((16, rows), I32)], 0),
        ],
        1,
    )
    packed = dot(halves.astype(F32).astype(BF), jnp.concatenate(places, 1)).astype(BF)
    for d in range(n_y):
        cd_b[d] = packed[:, d * LANES : (d + 1) * LANES]

    pl.semaphore_wait(barrier, n_xc + n_y + n_z - 3)
    for o in far_first(n_y):
        codes_out(o).start()

    centt_v[...] = (-cent_ref[...].astype(F32)).T.astype(BF)

    r128, l128 = iota((LANES, LANES), 0), iota((LANES, LANES), 1)
    rep = hot(iota((LANES, CODES), 0) % 16 == iota((LANES, CODES), 1) % 16)
    pick = iota((LANES, CODES), 0) % 16 == iota((LANES, CODES), 1) // 16
    fold = hot(iota((8, LANES), 1) // 16 == iota((8, LANES), 0))
    step = iota((LANES, rows), 0) % 16
    for g in range(SUB // 8):
        wide = jnp.concatenate(
            [jnp.broadcast_to(codes[g * 8 + j : g * 8 + j + 1], (16, rows)) for j in range(8)], 0
        )
        pairs = dot_nt(hot(wide // 16 == step), hot(wide % 16 == step))
        pairs = jnp.where(r128 // 16 == l128 // 16, pairs, 0.0).astype(BF)
        spread = jnp.where(pick, dot(pairs, rep), 0.0).astype(BF)
        tally = dot(fold, spread)
        for j in range(8):
            tl_v[j, g : g + 1] = tally[j : j + 1]
    for o in range(1, n_xc):
        tally1(o).start()

    for k in range(K_PARTS):
        for copy in loads[k]:
            copy.wait()
        part = dot(pooled_v[k], weight_v[k])
        if k == 0:
            res_v[...] = part
        else:
            res_v[...] += part
    acc = res_v[...]
    factor = lax.rsqrt(jnp.mean(acc * acc, axis=1, keepdims=True) + 1e-6)
    normed_v[...] = (acc * factor).astype(BF)

    group_list = target * CAP + slot
    ls_b[...] = dot(hot(iota((n_y * CAP, rows), 0) == group_list), normed_v[...]).astype(BF)
    ring(1, True).start()
    ring(1, False).start()

    xt_v[:, :rows] = normed_v[...].T
    call_v[:, :rows] = codes

    cd_r[0] = cd_b[y]
    for o in range(1, n_y):
        codes_out(o).wait_recv()
    low_lanes = iota((codes_half + 16, LANES), 1) < CAP
    picks = []
    members = jnp.zeros((CAP, LANES), F32)
    for p in range(n_y // 2):
        left, right = cd_r[2 * p].astype(F32), cd_r[2 * p + 1].astype(F32)
        upper = jnp.where(low_lanes, left, pltpu.roll(right, CAP, 1))
        lower = jnp.where(low_lanes, pltpu.roll(left, CAP, 1), right)
        cols = slice(rows + p * LANES, rows + (p + 1) * LANES)
        call_v[:codes_half, cols] = upper[:codes_half].astype(I32)
        call_v[codes_half:, cols] = lower[:codes_half].astype(I32)
        chosen = hot(iota((CAP, LANES), 0) + 1 == upper[codes_half : codes_half + 1].astype(I32))
        picks.append(chosen)
        members = members + chosen.astype(F32)
    xt_v[:, rows:] = dot(centt_v[...], jnp.concatenate(picks, 1)).astype(BF)
    tally_v[...] = jnp.broadcast_to(jnp.sum(members, axis=1, keepdims=True), (CAP, LANES))

    all_rows = call_v.shape[1]
    low = iota((16, all_rows), 0)

    def code_sums(o, out, kind):
        dest = lax.rem(xc + o, n_xc)
        for d in range(n_y):
            m = d * n_xc + dest
            gap = jnp.broadcast_to(call_v[pl.ds(m, 1)], (16, all_rows)) - low
            select = jnp.concatenate([hot(gap == 16 * h) for h in range(CODES // 16)], 0)
            piece = xt_v[pl.ds(pl.multiple_of(m * SUBW, SUBW), SUBW)]
            out[d * SUBW : (d + 1) * SUBW] = dot_nt(piece, select).astype(kind)

    def remote_chunks(offsets):
        for o in offsets:
            code_sums(o, s1_b.at[o], BF)
            sums1(o).start()

    order = far_first(n_xc)
    remote_chunks(order[:1])

    own = tl_v[xc]
    for o in range(1, n_xc):
        tally1(o).wait_recv()
        own = own + t1_r[o]
    for d in range(n_y):
        t2_b[d] = own[d : d + 1]
    for o in range(1, n_y):
        tally2(o).start()
    ring_step(2)
    remote_chunks(order[1:5])

    ring_step(3)
    remote_chunks(order[5:])
    code_sums(0, own_v, F32)

    for o in range(1, n_xc):
        sums1(o).wait_recv()
    for o in far_first(n_y) + [0]:
        d = at_y(o)
        part = pl.ds(pl.multiple_of(d * SUBW, SUBW), SUBW)
        run = own_v[part]
        for i in range(1, n_xc):
            run = run + s1_r[i, part].astype(F32)
        s2_b[d] = run
        if o:
            sums2(o).start()
    total = t2_b[y]
    for o in range(1, n_y):
        tally2(o).wait_recv()
        total = total + t2_r[o]
    t3_r[z] = total
    for o in range(1, n_z):
        tally3(o).start()
    run = s2_b[y]
    for o in range(1, n_y):
        sums2(o).wait_recv()
        run = run + s2_r[o]
    s3_r[z] = run.astype(BF)
    for o in range(1, n_z):
        sums3(o).start()
    for s in range(4, far + 1):
        ring_step(s)
    for o in range(1, n_z):
        tally3(o).wait_recv()
    for o in range(1, n_z):
        sums3(o).wait_recv()
    total, run = t3_r[0], s3_r[0].astype(F32)
    for i in range(1, n_z):
        total = total + t3_r[i]
        run = run + s3_r[i].astype(F32)
    s4_r[xc] = run / (1.0 + total)
    for o in far_first(n_xc):
        sums4(o).start()

    lists = cent_ref[...].astype(F32) + ls_b[block(0)].astype(F32)
    for up, slots in ((True, up_r), (False, down_r)):
        ring(far, up).wait_recv()
        lists = lists + slots[far - 1].astype(F32)
    newc_ref[...] = lists * (1.0 / (1.0 + tally_v[:, :1]))

    for o in range(1, n_xc):
        sums4(o).wait_recv()
    book_ref[...] = s4_r[...]

    for o in range(1, n_xc):
        tally1(o).wait_send()
        sums1(o).wait_send()
        sums4(o).wait_send()
    for o in range(1, n_y):
        codes_out(o).wait_send()
        tally2(o).wait_send()
        sums2(o).wait_send()
    for s in range(1, far + 1):
        ring(s, True).wait_send()
        ring(s, False).wait_send()
    for o in range(1, n_z):
        tally3(o).wait_send()
        sums3(o).wait_send()


def local(n_z, n_xc, pooled, proj_weight, centroids, list_slot, pq_codes, route_counts):
    n_y = lax.axis_size("lists")
    rows, din = pooled.shape
    features = proj_weight.shape[1]
    all_rows = rows + n_y * CAP
    far = n_y // 2
    share = SUB // n_y
    depth = din // K_PARTS
    sem = pltpu.SemaphoreType.DMA
    slots = list_slot.reshape(1, rows)
    operands = (route_counts, slots, pq_codes.T, centroids, pooled, proj_weight)
    vmem = pl.BlockSpec(memory_space=pltpu.VMEM)
    hbm = pl.BlockSpec(memory_space=pltpu.HBM)
    return pl.pallas_call(
        functools.partial(kernel, n_z, n_xc, n_y),
        out_shape=(
            jax.ShapeDtypeStruct(centroids.shape, F32),
            jax.ShapeDtypeStruct((share, SUBW, CODES), F32),
        ),
        in_specs=[hbm] * 6,
        out_specs=(vmem, vmem),
        scratch_shapes=[
            pltpu.SMEM((1, n_y), I32),
            pltpu.VMEM((1, rows), I32),
            pltpu.VMEM((SUB, rows), I32),
            pltpu.VMEM(centroids.shape, BF),
            pltpu.VMEM((K_PARTS, rows, depth), BF),
            pltpu.VMEM((K_PARTS, depth, features), BF),
            pltpu.VMEM((rows, features), BF),
            pltpu.VMEM((features, all_rows), BF),
            pltpu.VMEM((SUB, all_rows), I32),
            pltpu.VMEM((n_y * SUBW, CODES), F32),
            pltpu.VMEM((rows, features), F32),
            pltpu.VMEM((n_xc, n_y, CODES), F32),
            pltpu.VMEM((n_xc, n_y, CODES), F32),
            pltpu.VMEM((n_y, 1, CODES), F32),
            pltpu.VMEM((n_y, 1, CODES), F32),
            pltpu.VMEM((n_z, 1, CODES), F32),
            pltpu.VMEM((n_y, SUB // 2 + 16, LANES), BF),
            pltpu.VMEM((n_y, SUB // 2 + 16, LANES), BF),
            pltpu.VMEM((features, CAP), BF),
            pltpu.VMEM((n_y * CAP, features), BF),
            pltpu.VMEM((far, CAP, features), BF),
            pltpu.VMEM((far, CAP, features), BF),
            pltpu.VMEM((CAP, LANES), F32),
            pltpu.VMEM((n_xc, n_y * SUBW, CODES), BF),
            pltpu.VMEM((n_xc, n_y * SUBW, CODES), BF),
            pltpu.VMEM((n_y, SUBW, CODES), F32),
            pltpu.VMEM((n_y, SUBW, CODES), F32),
            pltpu.VMEM((n_z, SUBW, CODES), BF),
            pltpu.VMEM((n_xc, SUBW, CODES), F32),
            sem((2, K_PARTS)), sem((4,)), sem((2, n_xc)), sem((2, n_y)), sem((2, n_z)), sem((2, n_y)),
            sem((2, far)), sem((2, far)), sem((2, n_xc)), sem((2, n_y)),
            sem((2, n_z)), sem((2, n_xc)),
        ],
        compiler_params=pltpu.CompilerParams(
            collective_id=0, has_side_effects=True, vmem_limit_bytes=48 << 20
        ),
        name="step",
    )(*(pltpu.with_memory_space_constraint(v, pltpu.HBM) for v in operands))


def solution(mesh):
    n_xc = SUB // mesh.shape["lists"]
    in_specs = (
        P(("dp", "lists"), None),
        P(),
        P(("dp", "lists"), None),
        P(("dp", "lists")),
        P(("dp", "lists"), None),
        P(("dp", "lists"), None),
    )
    out_specs = (P(("dp", "lists"), None), P("lists", None, None))
    step = functools.partial(local, mesh.shape["dp"] // n_xc, n_xc)
    return jax.shard_map(step, mesh=mesh, in_specs=in_specs, out_specs=out_specs, check_vma=False)
```

```python
import functools

import jax
import jax.numpy as jnp
from jax import lax
from jax.experimental import pallas as pl
from jax.experimental.pallas import tpu as pltpu
from jax.sharding import PartitionSpec as P

SUB = 64
CODES = 256
SUBW = 16
CAP = 64
LANES = 128
MESH = pl.DeviceIdType.MESH
BF = jnp.bfloat16
F32 = jnp.float32
I32 = jnp.int32
K_PARTS = 4


def iota(shape, dim):
    return lax.broadcasted_iota(I32, shape, dim)


def hot(mask):
    return jnp.where(mask, 1.0, 0.0).astype(BF)


def dot(a, b):
    return jnp.dot(a, b, preferred_element_type=F32)


def dot_nt(a, b):
    return lax.dot_general(a, b, (((1,), (1,)), ((), ())), preferred_element_type=F32)


def far_first(n):
    return sorted(range(1, n), key=lambda o: -min(o, n - o))


def kernel(
    n_z, n_xc, n_y,
    counts_hbm, slot_hbm, codes_hbm, cent_hbm, pooled_hbm, weight_hbm,
    newc_ref, book_ref,
    counts_ref, slot_ref, codes_ref, cent_ref,
    pooled_v, weight_v, normed_v, xt_v, call_v, own_v, res_v,
    tl_v, t1_r, t2_b, t2_r, t3_r,
    cd_b, cd_r, centt_v, ls_b, up_r, down_r, tally_v, s1_b, s1_r, s2_b, s2_r, s3_r, s4_r,
    in_sem, small_sem, tl_s, t2_s, t3_s, cd_s, up_s, down_s, s1_s, s2_s, s3_s, s4_s,
):
    rows, features = normed_v.shape[0], res_v.shape[1]
    dp, y = lax.axis_index("dp"), lax.axis_index("lists")
    z, xc = dp // n_xc, dp % n_xc

    def at_xc(o):
        return z * n_xc + lax.rem(xc + o, n_xc)

    def at_y(o):
        return lax.rem(y + o, n_y)

    def at_z(o):
        return lax.rem(z + o, n_z) * n_xc + xc

    def send(src, dst, sems, o, device):
        return pltpu.make_async_remote_copy(
            src_ref=src, dst_ref=dst, send_sem=sems.at[0, o], recv_sem=sems.at[1, o],
            device_id=device, device_id_type=MESH,
        )

    def tally1(o):
        return send(tl_v.at[lax.rem(xc + o, n_xc)], t1_r.at[o], tl_s, o, (at_xc(o), y))

    def tally2(o):
        return send(t2_b.at[at_y(o)], t2_r.at[o], t2_s, o, (dp, at_y(o)))

    def codes_out(o):
        return send(cd_b.at[at_y(o)], cd_r.at[o], cd_s, o, (dp, at_y(o)))

    far = n_y // 2
    half = features // 2

    def block(o):
        return pl.ds(pl.multiple_of(at_y(o) * CAP, CAP), CAP)

    def ring(s, up):
        dest = block(far + 1 - s if up else n_y - far - 1 + s)
        slots, sems = (up_r, up_s) if up else (down_r, down_s)
        src, dst = ls_b.at[dest], slots.at[s - 1]
        if s == 1:
            cols = pl.ds(0 if up else half, half)
            src, dst = src.at[:, cols], dst.at[:, cols]
        return send(src, dst, sems, s - 1, (dp, at_y(1 if up else n_y - 1)))

    def ring_step(s):
        for up in (True, False):
            ring(s - 1, up).wait_recv()
            dest = block(far + 1 - s if up else n_y - far - 1 + s)
            cols = slice(0, features)
            if s == 2:
                cols = slice(0, half) if up else slice(half, features)
            came = (up_r if up else down_r)[s - 2, :, cols].astype(F32)
            ls_b[dest, cols] = (ls_b[dest, cols].astype(F32) + came).astype(BF)
            ring(s, up).start()

    def sums1(o):
        return send(s1_b.at[o], s1_r.at[o], s1_s, o, (at_xc(o), y))

    def sums2(o):
        return send(s2_b.at[at_y(o)], s2_r.at[o], s2_s, o, (dp, at_y(o)))

    def tally3(o):
        return send(t3_r.at[z], t3_r.at[z], t3_s, o, (at_z(o), y))

    def sums3(o):
        return send(s3_r.at[z], s3_r.at[z], s3_s, o, (at_z(o), y))

    def sums4(o):
        return send(s4_r.at[xc], s4_r.at[xc], s4_s, o, (at_xc(o), y))

    barrier = pltpu.get_barrier_semaphore()
    for o in far_first(n_y):
        pl.semaphore_signal(barrier, inc=1, device_id=(dp, at_y(o)), device_id_type=MESH)
    for o in far_first(n_xc):
        pl.semaphore_signal(barrier, inc=1, device_id=(at_xc(o), y), device_id_type=MESH)
    for o in range(1, n_z):
        pl.semaphore_signal(barrier, inc=1, device_id=(at_z(o), y), device_id_type=MESH)

    small = [
        pltpu.make_async_copy(src, dst, small_sem.at[i])
        for i, (src, dst) in enumerate(
            (
                (counts_hbm, counts_ref),
                (slot_hbm, slot_ref),
                (codes_hbm, codes_ref),
                (cent_hbm, cent_ref),
            )
        )
    ]
    for copy in small:
        copy.start()
    depth = weight_v.shape[1]
    loads = []
    for k in range(K_PARTS):
        cols = pl.ds(k * depth, depth)
        pair = (
            pltpu.make_async_copy(pooled_hbm.at[:, cols], pooled_v.at[k], in_sem.at[0, k]),
            pltpu.make_async_copy(weight_hbm.at[cols], weight_v.at[k], in_sem.at[1, k]),
        )
        for copy in pair:
            copy.start()
        loads.append(pair)

    for copy in small:
        copy.wait()
    slot = slot_ref[...]
    pos = iota((1, rows), 1)
    target = jnp.zeros((1, rows), I32)
    row = iota((2 * rows, LANES), 0)
    lane = iota((2 * rows, LANES), 1) - row // rows * CAP
    row = row % rows
    start = 0
    places = []
    for d in range(n_y):
        count = counts_ref[0, d]
        places.append(hot((row == lane + start) & (lane >= 0) & (lane < count)))
        start = start + count
        target = target + jnp.where(pos >= start, 1, 0)
    codes = codes_ref[...]
    codes_half = SUB // 2
    extra = jnp.where(iota((16, rows), 0) == 0, slot + 1, 0)
    halves = jnp.concatenate(
        [
            jnp.concatenate([codes[:codes_half], extra], 0),
            jnp.concatenate([codes[codes_half:], jnp.zeros((16, rows), I32)], 0),
        ],
        1,
    )
    packed = dot(halves.astype(F32).astype(BF), jnp.concatenate(places, 1)).astype(BF)
    for d in range(n_y):
        cd_b[d] = packed[:, d * LANES : (d + 1) * LANES]

    pl.semaphore_wait(barrier, n_xc + n_y + n_z - 3)
    for o in far_first(n_y):
        codes_out(o).start()

    centt_v[...] = (-cent_ref[...].astype(F32)).T.astype(BF)

    r128, l128 = iota((LANES, LANES), 0), iota((LANES, LANES), 1)
    rep = hot(iota((LANES, CODES), 0) % 16 == iota((LANES, CODES), 1) % 16)
    pick = iota((LANES, CODES), 0) % 16 == iota((LANES, CODES), 1) // 16
    fold = hot(iota((8, LANES), 1) // 16 == iota((8, LANES), 0))
    step = iota((LANES, rows), 0) % 16
    for g in range(SUB // 8):
        wide = jnp.concatenate(
            [jnp.broadcast_to(codes[g * 8 + j : g * 8 + j + 1], (16, rows)) for j in range(8)], 0
        )
        pairs = dot_nt(hot(wide // 16 == step), hot(wide % 16 == step))
        pairs = jnp.where(r128 // 16 == l128 // 16, pairs, 0.0).astype(BF)
        spread = jnp.where(pick, dot(pairs, rep), 0.0).astype(BF)
        tally = dot(fold, spread)
        for j in range(8):
            tl_v[j, g : g + 1] = tally[j : j + 1]
    for o in range(1, n_xc):
        tally1(o).start()

    for k in range(K_PARTS):
        for copy in loads[k]:
            copy.wait()
        part = dot(pooled_v[k], weight_v[k])
        if k == 0:
            res_v[...] = part
        else:
            res_v[...] += part
    acc = res_v[...]
    factor = lax.rsqrt(jnp.mean(acc * acc, axis=1, keepdims=True) + 1e-6)
    normed_v[...] = (acc * factor).astype(BF)

    group_list = target * CAP + slot
    ls_b[...] = dot(hot(iota((n_y * CAP, rows), 0) == group_list), normed_v[...]).astype(BF)
    ring(1, True).start()
    ring(1, False).start()

    xt_v[:, :rows] = normed_v[...].T
    call_v[:, :rows] = codes

    cd_r[0] = cd_b[y]
    for o in range(1, n_y):
        codes_out(o).wait_recv()
    low_lanes = iota((codes_half + 16, LANES), 1) < CAP
    picks = []
    members = jnp.zeros((CAP, LANES), F32)
    for p in range(n_y // 2):
        left, right = cd_r[2 * p].astype(F32), cd_r[2 * p + 1].astype(F32)
        upper = jnp.where(low_lanes, left, pltpu.roll(right, CAP, 1))
        lower = jnp.where(low_lanes, pltpu.roll(left, CAP, 1), right)
        cols = slice(rows + p * LANES, rows + (p + 1) * LANES)
        call_v[:codes_half, cols] = upper[:codes_half].astype(I32)
        call_v[codes_half:, cols] = lower[:codes_half].astype(I32)
        chosen = hot(iota((CAP, LANES), 0) + 1 == upper[codes_half : codes_half + 1].astype(I32))
        picks.append(chosen)
        members = members + chosen.astype(F32)
    xt_v[:, rows:] = dot(centt_v[...], jnp.concatenate(picks, 1)).astype(BF)
    tally_v[...] = jnp.broadcast_to(jnp.sum(members, axis=1, keepdims=True), (CAP, LANES))

    all_rows = call_v.shape[1]
    low = iota((16, all_rows), 0)

    def code_sums(o, out, kind):
        dest = lax.rem(xc + o, n_xc)
        for d in range(n_y):
            m = d * n_xc + dest
            gap = jnp.broadcast_to(call_v[pl.ds(m, 1)], (16, all_rows)) - low
            select = jnp.concatenate([hot(gap == 16 * h) for h in range(CODES // 16)], 0)
            piece = xt_v[pl.ds(pl.multiple_of(m * SUBW, SUBW), SUBW)]
            out[d * SUBW : (d + 1) * SUBW] = dot_nt(piece, select).astype(kind)

    def remote_chunks(offsets):
        for o in offsets:
            code_sums(o, s1_b.at[o], BF)
            sums1(o).start()

    order = far_first(n_xc)
    remote_chunks(order[:3])

    own = tl_v[xc]
    for o in range(1, n_xc):
        tally1(o).wait_recv()
        own = own + t1_r[o]
    for d in range(n_y):
        t2_b[d] = own[d : d + 1]
    for o in range(1, n_y):
        tally2(o).start()
    ring_step(2)
    remote_chunks(order[3:])

    code_sums(0, own_v, F32)

    for o in range(1, n_xc):
        sums1(o).wait_recv()
    for o in far_first(n_y) + [0]:
        d = at_y(o)
        part = pl.ds(pl.multiple_of(d * SUBW, SUBW), SUBW)
        run = own_v[part]
        for i in range(1, n_xc):
            run = run + s1_r[i, part].astype(F32)
        s2_b[d] = run
        if o:
            sums2(o).start()
    ring_step(3)
    total = t2_b[y]
    for o in range(1, n_y):
        tally2(o).wait_recv()
        total = total + t2_r[o]
    t3_r[z] = total
    for o in range(1, n_z):
        tally3(o).start()
    run = s2_b[y]
    for o in range(1, n_y):
        sums2(o).wait_recv()
        run = run + s2_r[o]
    s3_r[z] = run.astype(BF)
    for o in range(1, n_z):
        sums3(o).start()
    for s in range(4, far + 1):
        ring_step(s)
    for o in range(1, n_z):
        tally3(o).wait_recv()
    for o in range(1, n_z):
        sums3(o).wait_recv()
    total, run = t3_r[0], s3_r[0].astype(F32)
    for i in range(1, n_z):
        total = total + t3_r[i]
        run = run + s3_r[i].astype(F32)
    s4_r[xc] = run / (1.0 + total)
    for o in far_first(n_xc):
        sums4(o).start()

    lists = cent_ref[...].astype(F32) + ls_b[block(0)].astype(F32)
    for up, slots in ((True, up_r), (False, down_r)):
        ring(far, up).wait_recv()
        lists = lists + slots[far - 1].astype(F32)
    newc_ref[...] = lists * (1.0 / (1.0 + tally_v[:, :1]))

    for o in range(1, n_xc):
        sums4(o).wait_recv()
    book_ref[...] = s4_r[...]

    for o in range(1, n_xc):
        tally1(o).wait_send()
        sums1(o).wait_send()
        sums4(o).wait_send()
    for o in range(1, n_y):
        codes_out(o).wait_send()
        tally2(o).wait_send()
        sums2(o).wait_send()
    for s in range(1, far + 1):
        ring(s, True).wait_send()
        ring(s, False).wait_send()
    for o in range(1, n_z):
        tally3(o).wait_send()
        sums3(o).wait_send()


def local(n_z, n_xc, pooled, proj_weight, centroids, list_slot, pq_codes, route_counts):
    n_y = lax.axis_size("lists")
    rows, din = pooled.shape
    features = proj_weight.shape[1]
    all_rows = rows + n_y * CAP
    far = n_y // 2
    share = SUB // n_y
    depth = din // K_PARTS
    sem = pltpu.SemaphoreType.DMA
    slots = list_slot.reshape(1, rows)
    operands = (route_counts, slots, pq_codes.T, centroids, pooled, proj_weight)
    vmem = pl.BlockSpec(memory_space=pltpu.VMEM)
    hbm = pl.BlockSpec(memory_space=pltpu.HBM)
    return pl.pallas_call(
        functools.partial(kernel, n_z, n_xc, n_y),
        out_shape=(
            jax.ShapeDtypeStruct(centroids.shape, F32),
            jax.ShapeDtypeStruct((share, SUBW, CODES), F32),
        ),
        in_specs=[hbm] * 6,
        out_specs=(vmem, vmem),
        scratch_shapes=[
            pltpu.SMEM((1, n_y), I32),
            pltpu.VMEM((1, rows), I32),
            pltpu.VMEM((SUB, rows), I32),
            pltpu.VMEM(centroids.shape, BF),
            pltpu.VMEM((K_PARTS, rows, depth), BF),
            pltpu.VMEM((K_PARTS, depth, features), BF),
            pltpu.VMEM((rows, features), BF),
            pltpu.VMEM((features, all_rows), BF),
            pltpu.VMEM((SUB, all_rows), I32),
            pltpu.VMEM((n_y * SUBW, CODES), F32),
            pltpu.VMEM((rows, features), F32),
            pltpu.VMEM((n_xc, n_y, CODES), F32),
            pltpu.VMEM((n_xc, n_y, CODES), F32),
            pltpu.VMEM((n_y, 1, CODES), F32),
            pltpu.VMEM((n_y, 1, CODES), F32),
            pltpu.VMEM((n_z, 1, CODES), F32),
            pltpu.VMEM((n_y, SUB // 2 + 16, LANES), BF),
            pltpu.VMEM((n_y, SUB // 2 + 16, LANES), BF),
            pltpu.VMEM((features, CAP), BF),
            pltpu.VMEM((n_y * CAP, features), BF),
            pltpu.VMEM((far, CAP, features), BF),
            pltpu.VMEM((far, CAP, features), BF),
            pltpu.VMEM((CAP, LANES), F32),
            pltpu.VMEM((n_xc, n_y * SUBW, CODES), BF),
            pltpu.VMEM((n_xc, n_y * SUBW, CODES), BF),
            pltpu.VMEM((n_y, SUBW, CODES), F32),
            pltpu.VMEM((n_y, SUBW, CODES), F32),
            pltpu.VMEM((n_z, SUBW, CODES), BF),
            pltpu.VMEM((n_xc, SUBW, CODES), F32),
            sem((2, K_PARTS)), sem((4,)), sem((2, n_xc)), sem((2, n_y)), sem((2, n_z)), sem((2, n_y)),
            sem((2, far)), sem((2, far)), sem((2, n_xc)), sem((2, n_y)),
            sem((2, n_z)), sem((2, n_xc)),
        ],
        compiler_params=pltpu.CompilerParams(
            collective_id=0, has_side_effects=True, vmem_limit_bytes=48 << 20
        ),
        name="step",
    )(*(pltpu.with_memory_space_constraint(v, pltpu.HBM) for v in operands))


def solution(mesh):
    n_xc = SUB // mesh.shape["lists"]
    in_specs = (
        P(("dp", "lists"), None),
        P(),
        P(("dp", "lists"), None),
        P(("dp", "lists")),
        P(("dp", "lists"), None),
        P(("dp", "lists"), None),
    )
    out_specs = (P(("dp", "lists"), None), P("lists", None, None))
    step = functools.partial(local, mesh.shape["dp"] // n_xc, n_xc)
    return jax.shard_map(step, mesh=mesh, in_specs=in_specs, out_specs=out_specs, check_vma=False)
```

```python
import functools

import jax
import jax.numpy as jnp
from jax import lax
from jax.experimental import pallas as pl
from jax.experimental.pallas import tpu as pltpu
from jax.sharding import PartitionSpec as P

SUB = 64
CODES = 256
SUBW = 16
CAP = 64
LANES = 128
MESH = pl.DeviceIdType.MESH
BF = jnp.bfloat16
F32 = jnp.float32
I32 = jnp.int32
K_PARTS = 4


def iota(shape, dim):
    return lax.broadcasted_iota(I32, shape, dim)


def hot(mask):
    return jnp.where(mask, 1.0, 0.0).astype(BF)


def dot(a, b):
    return jnp.dot(a, b, preferred_element_type=F32)


def dot_nt(a, b):
    return lax.dot_general(a, b, (((1,), (1,)), ((), ())), preferred_element_type=F32)


def far_first(n):
    return sorted(range(1, n), key=lambda o: -min(o, n - o))


def kernel(
    n_z, n_xc, n_y,
    counts_hbm, slot_hbm, codes_hbm, cent_hbm, pooled_hbm, weight_hbm,
    newc_ref, book_ref,
    counts_ref, slot_ref, codes_ref, cent_ref,
    pooled_v, weight_v, normed_v, xt_v, call_v, own_v, res_v,
    tl_v, t1_r, t2_b, t2_r, t3_r,
    cd_b, cd_r, centt_v, ls_b, up_r, down_r, tally_v, s1_b, s1_r, s2_b, s2_r, s3_r, s4_r,
    in_sem, small_sem, tl_s, t2_s, t3_s, cd_s, up_s, down_s, s1_s, s2_s, s3_s, s4_s,
):
    rows, features = normed_v.shape[0], res_v.shape[1]
    dp, y = lax.axis_index("dp"), lax.axis_index("lists")
    z, xc = dp // n_xc, dp % n_xc

    def at_xc(o):
        return z * n_xc + lax.rem(xc + o, n_xc)

    def at_y(o):
        return lax.rem(y + o, n_y)

    def at_z(o):
        return lax.rem(z + o, n_z) * n_xc + xc

    def send(src, dst, sems, o, device):
        return pltpu.make_async_remote_copy(
            src_ref=src, dst_ref=dst, send_sem=sems.at[0, o], recv_sem=sems.at[1, o],
            device_id=device, device_id_type=MESH,
        )

    def tally1(o):
        return send(tl_v.at[lax.rem(xc + o, n_xc)], t1_r.at[o], tl_s, o, (at_xc(o), y))

    def tally2(o):
        return send(t2_b.at[at_y(o)], t2_r.at[o], t2_s, o, (dp, at_y(o)))

    def codes_out(o):
        return send(cd_b.at[at_y(o)], cd_r.at[o], cd_s, o, (dp, at_y(o)))

    far = n_y // 2
    half = features // 2

    def block(o):
        return pl.ds(pl.multiple_of(at_y(o) * CAP, CAP), CAP)

    def ring(s, up):
        dest = block(far + 1 - s if up else n_y - far - 1 + s)
        slots, sems = (up_r, up_s) if up else (down_r, down_s)
        src, dst = ls_b.at[dest], slots.at[s - 1]
        if s == 1:
            cols = pl.ds(0 if up else half, half)
            src, dst = src.at[:, cols], dst.at[:, cols]
        return send(src, dst, sems, s - 1, (dp, at_y(1 if up else n_y - 1)))

    def ring_step(s):
        for up in (True, False):
            ring(s - 1, up).wait_recv()
            dest = block(far + 1 - s if up else n_y - far - 1 + s)
            cols = slice(0, features)
            if s == 2:
                cols = slice(0, half) if up else slice(half, features)
            came = (up_r if up else down_r)[s - 2, :, cols].astype(F32)
            ls_b[dest, cols] = (ls_b[dest, cols].astype(F32) + came).astype(BF)
            ring(s, up).start()

    def sums1(o):
        return send(s1_b.at[o], s1_r.at[o], s1_s, o, (at_xc(o), y))

    def sums2(o):
        return send(s2_b.at[at_y(o)], s2_r.at[o], s2_s, o, (dp, at_y(o)))

    def tally3(o):
        return send(t3_r.at[z], t3_r.at[z], t3_s, o, (at_z(o), y))

    def sums3(o):
        return send(s3_r.at[z], s3_r.at[z], s3_s, o, (at_z(o), y))

    def sums4(o):
        return send(s4_r.at[xc], s4_r.at[xc], s4_s, o, (at_xc(o), y))

    barrier = pltpu.get_barrier_semaphore()
    for o in far_first(n_y):
        pl.semaphore_signal(barrier, inc=1, device_id=(dp, at_y(o)), device_id_type=MESH)
    for o in far_first(n_xc):
        pl.semaphore_signal(barrier, inc=1, device_id=(at_xc(o), y), device_id_type=MESH)
    for o in range(1, n_z):
        pl.semaphore_signal(barrier, inc=1, device_id=(at_z(o), y), device_id_type=MESH)

    small = [
        pltpu.make_async_copy(src, dst, small_sem.at[i])
        for i, (src, dst) in enumerate(
            (
                (counts_hbm, counts_ref),
                (slot_hbm, slot_ref),
                (codes_hbm, codes_ref),
                (cent_hbm, cent_ref),
            )
        )
    ]
    for copy in small:
        copy.start()
    depth = weight_v.shape[1]
    loads = []
    whole = pltpu.make_async_copy(pooled_hbm, pooled_v, in_sem.at[K_PARTS])
    whole.start()
    for k in range(K_PARTS):
        part = pl.ds(k * depth, depth)
        loads.append(pltpu.make_async_copy(weight_hbm.at[part], weight_v.at[k], in_sem.at[k]))
        loads[k].start()

    for copy in small:
        copy.wait()
    slot = slot_ref[...]
    pos = iota((1, rows), 1)
    target = jnp.zeros((1, rows), I32)
    row = iota((2 * rows, LANES), 0)
    lane = iota((2 * rows, LANES), 1) - row // rows * CAP
    row = row % rows
    start = 0
    places = []
    for d in range(n_y):
        count = counts_ref[0, d]
        places.append(hot((row == lane + start) & (lane >= 0) & (lane < count)))
        start = start + count
        target = target + jnp.where(pos >= start, 1, 0)
    codes = codes_ref[...]
    codes_half = SUB // 2
    extra = jnp.where(iota((16, rows), 0) == 0, slot + 1, 0)
    halves = jnp.concatenate(
        [
            jnp.concatenate([codes[:codes_half], extra], 0),
            jnp.concatenate([codes[codes_half:], jnp.zeros((16, rows), I32)], 0),
        ],
        1,
    )
    packed = dot(halves.astype(F32).astype(BF), jnp.concatenate(places, 1)).astype(BF)
    for d in range(n_y):
        cd_b[d] = packed[:, d * LANES : (d + 1) * LANES]

    pl.semaphore_wait(barrier, n_xc + n_y + n_z - 3)
    for o in far_first(n_y):
        codes_out(o).start()

    centt_v[...] = (-cent_ref[...].astype(F32)).T.astype(BF)

    r128, l128 = iota((LANES, LANES), 0), iota((LANES, LANES), 1)
    rep = hot(iota((LANES, CODES), 0) % 16 == iota((LANES, CODES), 1) % 16)
    pick = iota((LANES, CODES), 0) % 16 == iota((LANES, CODES), 1) // 16
    fold = hot(iota((8, LANES), 1) // 16 == iota((8, LANES), 0))
    step = iota((LANES, rows), 0) % 16
    for g in range(SUB // 8):
        wide = jnp.concatenate(
            [jnp.broadcast_to(codes[g * 8 + j : g * 8 + j + 1], (16, rows)) for j in range(8)], 0
        )
        pairs = dot_nt(hot(wide // 16 == step), hot(wide % 16 == step))
        pairs = jnp.where(r128 // 16 == l128 // 16, pairs, 0.0).astype(BF)
        spread = jnp.where(pick, dot(pairs, rep), 0.0).astype(BF)
        tally = dot(fold, spread)
        for j in range(8):
            tl_v[j, g : g + 1] = tally[j : j + 1]
    for o in range(1, n_xc):
        tally1(o).start()

    for k in range(K_PARTS):
        if k == 0:
            whole.wait()
        loads[k].wait()
        part = dot(pooled_v[:, k * depth : (k + 1) * depth], weight_v[k])
        if k == 0:
            res_v[...] = part
        else:
            res_v[...] += part
    acc = res_v[...]
    factor = lax.rsqrt(jnp.mean(acc * acc, axis=1, keepdims=True) + 1e-6)
    normed_v[...] = (acc * factor).astype(BF)

    group_list = target * CAP + slot
    ls_b[...] = dot(hot(iota((n_y * CAP, rows), 0) == group_list), normed_v[...]).astype(BF)
    ring(1, True).start()
    ring(1, False).start()

    xt_v[:, :rows] = normed_v[...].T
    call_v[:, :rows] = codes

    cd_r[0] = cd_b[y]
    for o in range(1, n_y):
        codes_out(o).wait_recv()
    low_lanes = iota((codes_half + 16, LANES), 1) < CAP
    picks = []
    members = jnp.zeros((CAP, LANES), F32)
    for p in range(n_y // 2):
        left, right = cd_r[2 * p].astype(F32), cd_r[2 * p + 1].astype(F32)
        upper = jnp.where(low_lanes, left, pltpu.roll(right, CAP, 1))
        lower = jnp.where(low_lanes, pltpu.roll(left, CAP, 1), right)
        cols = slice(rows + p * LANES, rows + (p + 1) * LANES)
        call_v[:codes_half, cols] = upper[:codes_half].astype(I32)
        call_v[codes_half:, cols] = lower[:codes_half].astype(I32)
        chosen = hot(iota((CAP, LANES), 0) + 1 == upper[codes_half : codes_half + 1].astype(I32))
        picks.append(chosen)
        members = members + chosen.astype(F32)
    xt_v[:, rows:] = dot(centt_v[...], jnp.concatenate(picks, 1)).astype(BF)
    tally_v[...] = jnp.broadcast_to(jnp.sum(members, axis=1, keepdims=True), (CAP, LANES))

    all_rows = call_v.shape[1]
    low = iota((16, all_rows), 0)

    def code_sums(o, out, kind):
        dest = lax.rem(xc + o, n_xc)
        for d in range(n_y):
            m = d * n_xc + dest
            gap = jnp.broadcast_to(call_v[pl.ds(m, 1)], (16, all_rows)) - low
            select = jnp.concatenate([hot(gap == 16 * h) for h in range(CODES // 16)], 0)
            piece = xt_v[pl.ds(pl.multiple_of(m * SUBW, SUBW), SUBW)]
            out[d * SUBW : (d + 1) * SUBW] = dot_nt(piece, select).astype(kind)

    def remote_chunks(offsets):
        for o in offsets:
            code_sums(o, s1_b.at[o], BF)
            sums1(o).start()

    order = far_first(n_xc)
    remote_chunks(order[:3])

    own = tl_v[xc]
    for o in range(1, n_xc):
        tally1(o).wait_recv()
        own = own + t1_r[o]
    for d in range(n_y):
        t2_b[d] = own[d : d + 1]
    for o in range(1, n_y):
        tally2(o).start()
    ring_step(2)
    remote_chunks(order[3:])

    code_sums(0, own_v, F32)

    for o in range(1, n_xc):
        sums1(o).wait_recv()
    for o in far_first(n_y) + [0]:
        d = at_y(o)
        part = pl.ds(pl.multiple_of(d * SUBW, SUBW), SUBW)
        run = own_v[part]
        for i in range(1, n_xc):
            run = run + s1_r[i, part].astype(F32)
        s2_b[d] = run
        if o:
            sums2(o).start()
    ring_step(3)
    total = t2_b[y]
    for o in range(1, n_y):
        tally2(o).wait_recv()
        total = total + t2_r[o]
    t3_r[z] = total
    for o in range(1, n_z):
        tally3(o).start()
    run = s2_b[y]
    for o in range(1, n_y):
        sums2(o).wait_recv()
        run = run + s2_r[o]
    s3_r[z] = run.astype(BF)
    for o in range(1, n_z):
        sums3(o).start()
    for s in range(4, far + 1):
        ring_step(s)
    for o in range(1, n_z):
        tally3(o).wait_recv()
    for o in range(1, n_z):
        sums3(o).wait_recv()
    total, run = t3_r[0], s3_r[0].astype(F32)
    for i in range(1, n_z):
        total = total + t3_r[i]
        run = run + s3_r[i].astype(F32)
    s4_r[xc] = run / (1.0 + total)
    for o in far_first(n_xc):
        sums4(o).start()

    lists = cent_ref[...].astype(F32) + ls_b[block(0)].astype(F32)
    for up, slots in ((True, up_r), (False, down_r)):
        ring(far, up).wait_recv()
        lists = lists + slots[far - 1].astype(F32)
    newc_ref[...] = lists * (1.0 / (1.0 + tally_v[:, :1]))

    for o in range(1, n_xc):
        sums4(o).wait_recv()
    book_ref[...] = s4_r[...]

    for o in range(1, n_xc):
        tally1(o).wait_send()
        sums1(o).wait_send()
        sums4(o).wait_send()
    for o in range(1, n_y):
        codes_out(o).wait_send()
        tally2(o).wait_send()
        sums2(o).wait_send()
    for s in range(1, far + 1):
        ring(s, True).wait_send()
        ring(s, False).wait_send()
    for o in range(1, n_z):
        tally3(o).wait_send()
        sums3(o).wait_send()


def local(n_z, n_xc, pooled, proj_weight, centroids, list_slot, pq_codes, route_counts):
    n_y = lax.axis_size("lists")
    rows, din = pooled.shape
    features = proj_weight.shape[1]
    all_rows = rows + n_y * CAP
    far = n_y // 2
    share = SUB // n_y
    depth = din // K_PARTS
    sem = pltpu.SemaphoreType.DMA
    slots = list_slot.reshape(1, rows)
    operands = (route_counts, slots, pq_codes.T, centroids, pooled, proj_weight)
    vmem = pl.BlockSpec(memory_space=pltpu.VMEM)
    hbm = pl.BlockSpec(memory_space=pltpu.HBM)
    return pl.pallas_call(
        functools.partial(kernel, n_z, n_xc, n_y),
        out_shape=(
            jax.ShapeDtypeStruct(centroids.shape, F32),
            jax.ShapeDtypeStruct((share, SUBW, CODES), F32),
        ),
        in_specs=[hbm] * 6,
        out_specs=(vmem, vmem),
        scratch_shapes=[
            pltpu.SMEM((1, n_y), I32),
            pltpu.VMEM((1, rows), I32),
            pltpu.VMEM((SUB, rows), I32),
            pltpu.VMEM(centroids.shape, BF),
            pltpu.VMEM((rows, din), BF),
            pltpu.VMEM((K_PARTS, depth, features), BF),
            pltpu.VMEM((rows, features), BF),
            pltpu.VMEM((features, all_rows), BF),
            pltpu.VMEM((SUB, all_rows), I32),
            pltpu.VMEM((n_y * SUBW, CODES), F32),
            pltpu.VMEM((rows, features), F32),
            pltpu.VMEM((n_xc, n_y, CODES), F32),
            pltpu.VMEM((n_xc, n_y, CODES), F32),
            pltpu.VMEM((n_y, 1, CODES), F32),
            pltpu.VMEM((n_y, 1, CODES), F32),
            pltpu.VMEM((n_z, 1, CODES), F32),
            pltpu.VMEM((n_y, SUB // 2 + 16, LANES), BF),
            pltpu.VMEM((n_y, SUB // 2 + 16, LANES), BF),
            pltpu.VMEM((features, CAP), BF),
            pltpu.VMEM((n_y * CAP, features), BF),
            pltpu.VMEM((far, CAP, features), BF),
            pltpu.VMEM((far, CAP, features), BF),
            pltpu.VMEM((CAP, LANES), F32),
            pltpu.VMEM((n_xc, n_y * SUBW, CODES), BF),
            pltpu.VMEM((n_xc, n_y * SUBW, CODES), BF),
            pltpu.VMEM((n_y, SUBW, CODES), F32),
            pltpu.VMEM((n_y, SUBW, CODES), F32),
            pltpu.VMEM((n_z, SUBW, CODES), BF),
            pltpu.VMEM((n_xc, SUBW, CODES), F32),
            sem((K_PARTS + 1,)), sem((4,)), sem((2, n_xc)), sem((2, n_y)), sem((2, n_z)), sem((2, n_y)),
            sem((2, far)), sem((2, far)), sem((2, n_xc)), sem((2, n_y)),
            sem((2, n_z)), sem((2, n_xc)),
        ],
        compiler_params=pltpu.CompilerParams(
            collective_id=0, has_side_effects=True, vmem_limit_bytes=48 << 20
        ),
        name="step",
    )(*(pltpu.with_memory_space_constraint(v, pltpu.HBM) for v in operands))


def solution(mesh):
    n_xc = SUB // mesh.shape["lists"]
    in_specs = (
        P(("dp", "lists"), None),
        P(),
        P(("dp", "lists"), None),
        P(("dp", "lists")),
        P(("dp", "lists"), None),
        P(("dp", "lists"), None),
    )
    out_specs = (P(("dp", "lists"), None), P("lists", None, None))
    step = functools.partial(local, mesh.shape["dp"] // n_xc, n_xc)
    return jax.shard_map(step, mesh=mesh, in_specs=in_specs, out_specs=out_specs, check_vma=False)
```
